32 devices in a mesh: mem: 4 (over z), head: 2 (over y), span: 4 (over x, core).
Axes of the slice: x: 2, y: 2, z: 4, core: 2. Of those that a mesh axis runs over, the one named last changes fastest.
Arguments:
- query: bfloat16 [4, 512, 8, 8, 128], P('span', 'mem', 'head'), may hold values from -6 to 6
- new_keys: bfloat16 [4, 512, 8, 128], P('span', 'mem', 'head'), may hold values from -6 to 6
- new_values: bfloat16 [4, 512, 8, 128], P('span', 'mem', 'head'), may hold values from -5 to 5
- memory_keys: bfloat16 [128, 128, 8, 128], P('mem', None, 'head'), may hold values from -5 to 5
- memory_values: bfloat16 [128, 128, 8, 128], P('mem', None, 'head'), may hold values from -5 to 5
- retrieved: int32 [4, 8, 16], P('span', 'head'), may hold values from 0 to 127, as said below
Outputs:
- attended: bfloat16 [4, 512, 8192], P('span', ('mem', 'head'))
The draws below stay inside these ranges and needn't reach their ends.
Inputs may be any that keep to these rules, and one draw needn't show every extreme that they name: Each list retrieved[b, h, :] names 16 different units. The units o * 32 to (o + 1) * 32 - 1 appear at most 8 times in one list, and in every list some o has exactly 8.
All inputs are finite; a program needn't handle non-finite values.
Results may differ from the reference program's by a relative error of at most 0.005.
Values may be sent and summed in bfloat16 or wider, within the bound.
No kernel may reach another device: no remote copies, remote signals or barrier semaphores. Data moves between devices by JAX's collectives and lax.ppermute only.
A program may use at most 64 MiB of HBM per device.

```python
import math
import jax
import jax.numpy as jnp
from jax import lax

KVH = 8
HD = 128
UNIT = 128
TOPK = 16
UNITS_DEV = 32
QPK = 8
NBLOCKS = 4
BLOCK_LEN = 512
UNITS = 128
CAP = 8
N_MEM = 4


def draw_query(key, part):
    shape = (NBLOCKS, BLOCK_LEN, KVH, QPK, HD)
    base_key = jax.random.fold_in(key, 11)
    values = 2.0 * jax.random.truncated_normal(base_key, -3.0, 3.0, shape)
    return values.astype(jnp.bfloat16)


def draw_new_keys(key, part):
    shape = (NBLOCKS, BLOCK_LEN, KVH, HD)
    base_key = jax.random.fold_in(key, 13)
    values = jax.random.truncated_normal(base_key, -4.0, 4.0, shape)
    return values.astype(jnp.bfloat16)


def draw_retrieved(key, part):
    pair_count = N_MEM * CAP
    owner_of = jnp.arange(pair_count) // CAP
    slot_of = jnp.arange(pair_count) % CAP

    def unit_order(unit_key):
        return jax.random.permutation(unit_key, UNITS_DEV)[:CAP]

    def one_list(list_key):
        hot_key, order_key, unit_key = jax.random.split(list_key, 3)
        hot_owner = jax.random.randint(hot_key, (), 0, N_MEM)
        ranking = jax.random.permutation(order_key, pair_count)
        ranking = jnp.where(owner_of == hot_owner, ranking + pair_count, ranking)
        _, picked = lax.top_k(ranking, TOPK)
        local_pick = jax.vmap(unit_order)(jax.random.split(unit_key, N_MEM))
        units = owner_of * UNITS_DEV + local_pick[owner_of, slot_of]
        return units[picked].astype(jnp.int32)
    list_keys = jax.random.split(jax.random.fold_in(key, 17), NBLOCKS * KVH)
    return jax.vmap(one_list)(list_keys).reshape(NBLOCKS, KVH, TOPK)


def level_of(key, dims, pieces, least, high):
    gain = 1.0
    for dim, blocks in pieces:
        heights = jax.random.uniform(jax.random.fold_in(jax.random.fold_in(key, 6), dim), (blocks,), jnp.float32, least / len(pieces), high / len(pieces))
        gain = gain * jnp.repeat(jnp.exp(heights), dims[dim] // blocks).reshape((-1,) + (1,) * (len(dims) - 1 - dim))
    return gain


def bell_draw(own_key, shape, deviation, most, pieces=(), kind=jnp.bfloat16):
    drawn = jax.random.normal(own_key, shape, jnp.float32) * deviation
    if len(pieces) > 0:
        drawn = level_of(own_key, shape, pieces, -0.22, 0.18) * drawn
    return jnp.clip(drawn, min=-most, max=most).astype(kind)


def setup_inputs(seed: int = 0) -> dict:
    arg_keys = jax.random.split(jax.random.key(seed), 7)
    return {
        "query": draw_query(jax.random.fold_in(arg_keys[6], 71), 0),
        "new_keys": draw_new_keys(jax.random.fold_in(arg_keys[6], 71), 0),
        "new_values": bell_draw(arg_keys[2], (NBLOCKS, BLOCK_LEN, KVH, HD), 1.0, 5.0, ((0, 4), (1, 4), (2, 2))),
        "memory_keys": bell_draw(arg_keys[3], (UNITS, UNIT, KVH, HD), 1.0, 5.0, ((0, 4), (2, 2))),
        "memory_values": bell_draw(arg_keys[4], (UNITS, UNIT, KVH, HD), 1.0, 5.0, ((0, 4), (2, 2))),
        "retrieved": draw_retrieved(jax.random.fold_in(arg_keys[6], 71), 0),
    }


NEG = -1e+30

def reference(query, new_keys, new_values, memory_keys, memory_values, retrieved):
    score_scale = 1.0 / math.sqrt(HD)
    positions = jnp.arange(BLOCK_LEN, dtype=jnp.int32)
    causal = positions[None, :] <= positions[:, None]
    after = positions[None, :] > positions[:, None]

    def one_item(work_item):
        block_at = work_item // KVH
        head_at = work_item % KVH
        prior_at = jnp.maximum(block_at - 1, 0)
        queries = lax.dynamic_index_in_dim(lax.dynamic_index_in_dim(query, block_at, 0, False), head_at, 1, False)

        def pick(source, index_at):
            return lax.dynamic_index_in_dim(lax.dynamic_index_in_dim(source, index_at, 0, False), head_at, 1, False)
        unit_ids = lax.dynamic_index_in_dim(lax.dynamic_index_in_dim(retrieved, block_at, 0, False), head_at, 0, False)
        unit_keys = lax.dynamic_index_in_dim(memory_keys[unit_ids], head_at, 2, False).reshape(TOPK * UNIT, HD)
        unit_values = lax.dynamic_index_in_dim(memory_values[unit_ids], head_at, 2, False).reshape(TOPK * UNIT, HD)
        all_keys = jnp.concatenate([pick(new_keys, prior_at), pick(new_keys, block_at), unit_keys], axis=0)
        all_values = jnp.concatenate([pick(new_values, prior_at), pick(new_values, block_at), unit_values], axis=0)
        full_mask = jnp.concatenate([after & (block_at > 0), causal, jnp.ones((BLOCK_LEN, TOPK * UNIT), bool)], axis=1)
        scores = jnp.einsum('iqd,kd->iqk', queries.astype(jnp.float32), all_keys.astype(jnp.float32)) * score_scale
        scores = jnp.where(full_mask[:, None, :], scores, NEG)
        peak = lax.optimization_barrier(jnp.max(scores, axis=-1, keepdims=True))
        weights = jnp.where(full_mask[:, None, :], jnp.exp(scores - peak), 0.0)
        total = lax.optimization_barrier(jnp.sum(weights, axis=-1))
        rounded = lax.optimization_barrier(weights.astype(jnp.bfloat16)).astype(jnp.float32)
        summed = jnp.einsum('iqk,kd->iqd', rounded, all_values.astype(jnp.float32))
        return (summed / total[..., None]).astype(jnp.bfloat16)
    results = lax.map(one_item, jnp.arange(NBLOCKS * KVH, dtype=jnp.int32))
    results = results.reshape(NBLOCKS, KVH, BLOCK_LEN, QPK * HD)
    return jnp.transpose(results, (0, 2, 1, 3)).reshape(NBLOCKS, BLOCK_LEN, KVH * QPK * HD)
```

```python
import functools
import math

import jax
import jax.numpy as jnp
from jax import lax
from jax.experimental import pallas as pl
from jax.experimental.pallas import tpu as pltpu
from jax.sharding import PartitionSpec as P

NEG = -1e30
LANES = 256
VMEM = 56 * 1024 * 1024

PIECES = (8, 8, 16)
CHUNKS = (8, 24, 32)


def spec_smem():
    return pl.BlockSpec(memory_space=pltpu.SMEM)


def spec_vmem():
    return pl.BlockSpec(memory_space=pltpu.VMEM)


def spec_any():
    return pl.BlockSpec(memory_space=pl.ANY)


OWN, END, SEND, RECV, COUNT = range(5)
OFFSET = 64


def plan_kernel(units_dev, first, who_ref, list_ref, plan_ref):
    heads, topk = list_ref.shape
    width = plan_ref.shape[1]
    me, end, opp_mid, opp_end = (who_ref[index] for index in range(4))

    def clear(at, _):
        plan_ref[SEND, at] = -1
        plan_ref[RECV, at] = -1
        plan_ref[OWN, at] = 0
        plan_ref[END, at] = -1
        return 0

    lax.fori_loop(0, width, clear, 0)

    def walk(at, counts):
        head = at // topk
        unit = list_ref[head, at % topk]
        owner = unit // units_dev
        n_own, n_end, n_mid, n_far = counts

        @pl.when(owner == me)
        def _():
            plan_ref[OWN, n_own] = (unit % units_dev) * heads + head
            plan_ref[SEND, n_own] = n_own

        @pl.when(owner == end)
        def _():
            plan_ref[END, n_end] = head

        @pl.when(owner == opp_mid)
        def _():
            plan_ref[RECV, n_mid] = head

        return (
            n_own + (owner == me).astype(jnp.int32),
            n_end + (owner == end).astype(jnp.int32),
            n_mid + (owner == opp_mid).astype(jnp.int32),
            n_far + (owner == opp_end).astype(jnp.int32),
        )

    zero = jnp.int32(0)
    n_own, n_end, n_mid, n_far = lax.fori_loop(0, heads * topk, walk, (zero, zero, zero, zero))
    send_base = jnp.maximum(n_own, first)
    recv_base = jnp.maximum(n_mid, first)

    def forward(at, _):
        plan_ref[SEND, send_base + at] = OFFSET + at
        return 0

    lax.fori_loop(0, n_end, forward, 0)

    def tail(at, slot):
        head = at // topk
        here = (list_ref[head, at % topk] // units_dev) == opp_end

        @pl.when(here)
        def _():
            plan_ref[RECV, recv_base + slot] = head

        return slot + here.astype(jnp.int32)

    lax.fori_loop(0, heads * topk, tail, zero)
    plan_ref[COUNT, 0] = n_own
    plan_ref[COUNT, 1] = n_end
    plan_ref[COUNT, 2] = recv_base + n_far


def make_plan(who, unit_lists, units_dev, first):
    return pl.pallas_call(
        functools.partial(plan_kernel, units_dev, first),
        out_shape=jax.ShapeDtypeStruct((5, 128), jnp.int32),
        in_specs=[spec_smem(), spec_smem()],
        out_specs=spec_smem(),
    )(who, unit_lists)


def gather_kernel(first, plan_ref, keys_ref, values_ref, out_ref):
    slot = first + pl.program_id(0)
    rows, width = keys_ref.shape[1:]
    tokens = out_ref.shape[2]
    heads = rows // tokens

    @pl.when(slot < plan_ref[COUNT, 0])
    def _():
        head = plan_ref[OWN, slot] % heads
        token = lax.broadcasted_iota(jnp.int32, (tokens, rows), 0)
        row = lax.broadcasted_iota(jnp.int32, (tokens, rows), 1)
        pick = (row == token * heads + head).astype(jnp.bfloat16)
        out_ref[0, 0] = jnp.dot(
            pick, keys_ref[0], preferred_element_type=jnp.float32
        ).astype(jnp.bfloat16)
        out_ref[0, 1] = lax.dot_general(
            values_ref[0], pick, (((0,), (1,)), ((), ())), preferred_element_type=jnp.float32
        ).astype(jnp.bfloat16)


def gather(plan, keys, values, tokens, first, count):
    units, rows, width = keys.shape
    heads = rows // tokens

    def unit_at(step, plan_ref):
        return (plan_ref[OWN, first + step] // heads, 0, 0)

    return pl.pallas_call(
        functools.partial(gather_kernel, first),
        out_shape=jax.ShapeDtypeStruct((count, 2, tokens, width), jnp.bfloat16),
        grid_spec=pltpu.PrefetchScalarGridSpec(
            num_scalar_prefetch=1,
            grid=(count,),
            in_specs=[pl.BlockSpec((1, rows, width), unit_at)] * 2,
            out_specs=pl.BlockSpec((1, 2, tokens, width), lambda step, plan_ref: (step, 0, 0, 0)),
        ),
    )(plan, keys, values)


def pack_kernel(first, count, piece_sizes, plan_ref, *refs):
    n_piece = len(piece_sizes)
    own_refs, end_refs = refs[:n_piece], refs[n_piece : 2 * n_piece]
    out_ref, sems = refs[2 * n_piece :]

    def each(act):
        for slot in range(count):
            source = plan_ref[SEND, first + slot]
            base = 0
            for size, own_ref, end_ref in zip(piece_sizes, own_refs, end_refs):
                for offset, ref in ((0, own_ref), (OFFSET, end_ref)):
                    at = source - offset - base

                    @pl.when((at >= 0) & (at < size))
                    def _(ref=ref, at=at, slot=slot):
                        act(pltpu.make_async_copy(ref.at[at], out_ref.at[slot], sems.at[slot]))

                base += size

    each(lambda copy: copy.start())
    each(lambda copy: copy.wait())


def pack(plan, own, end, first, count):
    sizes = tuple(piece.shape[0] for piece in own)
    return pl.pallas_call(
        functools.partial(pack_kernel, first, count, sizes),
        out_shape=jax.ShapeDtypeStruct((count,) + own[0].shape[1:], jnp.bfloat16),
        in_specs=[spec_smem()] + [spec_any()] * (2 * len(own)),
        out_specs=spec_any(),
        scratch_shapes=[pltpu.SemaphoreType.DMA((count,))],
    )(plan, *own, *end)


def attend(scale, keys, values_t, queries_t, mask, state):
    peak, total, accum = state
    scores = jnp.dot(keys, queries_t, preferred_element_type=jnp.float32)
    if mask is not None:
        scores = jnp.where(mask, scores, NEG)
    new_peak = jnp.maximum(peak, jnp.max(scores, axis=0, keepdims=True))
    weights = jnp.exp2((scores - new_peak) * scale)
    factor = jnp.exp2((peak - new_peak) * scale)
    total = total * factor + jnp.sum(weights, axis=0, keepdims=True)
    accum = accum * factor + jnp.dot(
        values_t, weights.astype(jnp.bfloat16), preferred_element_type=jnp.float32
    )
    return new_peak, total, accum


def new_kernel(scale, who_ref, cur_ref, prior_ref, own_ref, end_ref, peak_ref, total_ref, accum_ref):
    low, has_prior, is_mid = who_ref[4] == 1, who_ref[5] == 1, who_ref[6] == 1
    tokens = cur_ref.shape[3]
    rows = own_ref.shape[2]

    def masks():
        key = lax.broadcasted_iota(jnp.int32, (tokens, LANES), 0)
        position = lax.broadcasted_iota(jnp.int32, (tokens, LANES), 1) % tokens
        return key <= position, (key > position) & has_prior

    @pl.when(is_mid)
    def _():
        for group, (query_ref, diagonal, others) in enumerate(
            ((own_ref, 0, ((1, True), (2, False), (3, False))), (end_ref, 1, ((0, False), (2, False), (3, False))))
        ):
            for start in range(0, rows, LANES):
                lanes = pl.ds(start, LANES)
                state_lanes = pl.ds(group * rows + start, LANES)
                queries_t = query_ref[0, :, lanes]
                state = (
                    jnp.full((1, LANES), NEG, jnp.float32),
                    jnp.zeros((1, LANES), jnp.float32),
                    jnp.zeros((cur_ref.shape[4], LANES), jnp.float32),
                )
                causal, after = masks()
                state = attend(
                    scale, cur_ref[diagonal, 0, 0], cur_ref[diagonal, 0, 1], queries_t, causal, state
                )
                state = attend(
                    scale, prior_ref[diagonal, 0, 0], prior_ref[diagonal, 0, 1], queries_t, after, state
                )
                peak_ref[0, :, state_lanes], total_ref[0, :, state_lanes], accum_ref[0, :, state_lanes] = state
            for tile, low_is_cur in others:
                is_cur = low == low_is_cur

                @pl.when(is_cur | has_prior)
                def _(tile=tile, is_cur=is_cur, group=group, query_ref=query_ref):
                    keys = jnp.where(is_cur, cur_ref[tile, 0, 0], prior_ref[tile, 0, 0])
                    values_t = jnp.where(is_cur, cur_ref[tile, 0, 1], prior_ref[tile, 0, 1])
                    for start in range(0, rows, LANES):
                        lanes = pl.ds(start, LANES)
                        state_lanes = pl.ds(group * rows + start, LANES)
                        state = (
                            peak_ref[0, :, state_lanes],
                            total_ref[0, :, state_lanes],
                            accum_ref[0, :, state_lanes],
                        )
                        state = attend(scale, keys, values_t, query_ref[0, :, lanes], None, state)
                        peak_ref[0, :, state_lanes], total_ref[0, :, state_lanes], accum_ref[0, :, state_lanes] = state


def attend_new(scale, who, cur, prior, own_t, end_t):
    tiles, heads, _, tokens, width = cur.shape
    rows = own_t.shape[2]
    kv_spec = pl.BlockSpec((tiles, 1, 2, tokens, width), lambda head: (0, head, 0, 0, 0))
    query_spec = pl.BlockSpec((1, width, rows), lambda head: (head, 0, 0))
    stat_spec = pl.BlockSpec((1, 1, 2 * rows), lambda head: (head, 0, 0))
    return pl.pallas_call(
        functools.partial(new_kernel, scale),
        grid=(heads,),
        out_shape=(
            jax.ShapeDtypeStruct((heads, 1, 2 * rows), jnp.float32),
            jax.ShapeDtypeStruct((heads, 1, 2 * rows), jnp.float32),
            jax.ShapeDtypeStruct((heads, width, 2 * rows), jnp.float32),
        ),
        in_specs=[spec_smem(), kv_spec, kv_spec, query_spec, query_spec],
        out_specs=(stat_spec, stat_spec, pl.BlockSpec((1, width, 2 * rows), lambda head: (head, 0, 0))),
        compiler_params=pltpu.CompilerParams(vmem_limit_bytes=VMEM),
        cost_estimate=pl.CostEstimate(flops=4 * 10 * tokens * heads * rows * width, bytes_accessed=10**7, transcendentals=0),
    )(who, cur, prior, own_t, end_t)


def units_kernel(scale, layout, last, who_ref, plan_ref, own_ref, end_ref, *refs):
    n_buffer = len(layout)
    buffers = refs[:n_buffer]
    peak_in, total_in, accum_in = refs[n_buffer : n_buffer + 3]
    outs = refs[n_buffer + 3 :]
    if last:
        out_own, out_end, peak_ref, total_ref, accum_ref = outs
    else:
        peak_ref, total_ref, accum_ref = outs
    rows = own_ref.shape[2]
    heads = own_ref.shape[0]

    @pl.when(who_ref[6] == 1)
    def _():
        peak_ref[...] = peak_in[...]
        total_ref[...] = total_in[...]
        accum_ref[...] = accum_in[...]
        for (kind, first), buffer in zip(layout, buffers):

            def item(slot, _, kind=kind, first=first, buffer=buffer):
                if kind == OWN:
                    head = plan_ref[OWN, first + slot] % heads
                else:
                    head = plan_ref[kind, first + slot]

                @pl.when(head >= 0)
                def _():
                    keys, values_t = buffer[slot, 0], buffer[slot, 1]
                    for group, query_ref in enumerate((own_ref, end_ref)):
                        for start in range(0, rows, LANES):
                            state_lanes = pl.ds(group * rows + start, LANES)
                            state = (
                                peak_ref[head, :, state_lanes],
                                total_ref[head, :, state_lanes],
                                accum_ref[head, :, state_lanes],
                            )
                            state = attend(
                                scale, keys, values_t, query_ref[head, :, pl.ds(start, LANES)], None, state
                            )
                            (
                                peak_ref[head, :, state_lanes],
                                total_ref[head, :, state_lanes],
                                accum_ref[head, :, state_lanes],
                            ) = state

                return 0

            size = buffer.shape[0]
            if kind == RECV:
                used = plan_ref[COUNT, 2]
            else:
                used = plan_ref[COUNT, 0 if kind == OWN else 1]
            lax.fori_loop(0, jnp.clip(used - first, 0, size), item, 0)
        if last:
            tokens, width = out_own.shape[0], accum_ref.shape[1]
            group_size = rows // tokens
            for group, out_ref in enumerate((out_own, out_end)):
                for head in range(heads):
                    for member in range(group_size):
                        lanes = pl.ds(group * rows + member * tokens, tokens)
                        result = accum_ref[head, :, lanes] / total_ref[head, :, lanes]
                        out_ref[:, pl.ds((head * group_size + member) * width, width)] = (
                            result.T.astype(jnp.bfloat16)
                        )


def attend_units(scale, who, plan, own_t, end_t, buffers, state, last, tokens):
    layout = tuple((kind, first) for kind, first, _ in buffers)
    arrays = [array for _, _, array in buffers]
    heads, width, rows = own_t.shape
    state_shapes = [jax.ShapeDtypeStruct(part.shape, part.dtype) for part in state]
    outs = []
    scratch = []
    if last:
        outs = [jax.ShapeDtypeStruct((tokens, heads * rows // tokens * width), jnp.bfloat16)] * 2
        scratch = [pltpu.VMEM(part.shape, part.dtype) for part in state]
    else:
        outs = state_shapes
    n_units = sum(array.shape[0] for array in arrays)
    return pl.pallas_call(
        functools.partial(units_kernel, scale, layout, last),
        out_shape=tuple(outs),
        in_specs=[spec_smem(), spec_smem()] + [spec_vmem()] * (2 + len(arrays) + 3),
        out_specs=tuple([spec_vmem()] * len(outs)),
        scratch_shapes=scratch,
        compiler_params=pltpu.CompilerParams(vmem_limit_bytes=VMEM),
        cost_estimate=pl.CostEstimate(
            flops=8 * n_units * 128 * rows * width, bytes_accessed=10**7, transcendentals=0
        ),
    )(who, plan, own_t, end_t, *arrays, *state)


def line_of_four(query, new_keys, new_values, memory_keys, memory_values, retrieved):
    queries = query[0]
    tokens, heads, group_size, width = queries.shape
    units_dev = memory_keys.shape[0]
    scale = math.log2(math.e) / math.sqrt(width)
    me = lax.axis_index("mem")
    span = lax.axis_index("span")
    low = (me < 2).astype(jnp.int32)
    is_mid = ((me == 1) | (me == 2)).astype(jnp.int32)
    end = jnp.where(low == 1, 0, 3)
    who = jnp.stack(
        [me, end, 3 - me, 3 - end, low, (span > 0).astype(jnp.int32), is_mid, jnp.int32(0)]
    ).astype(jnp.int32)

    def inward(value):
        return lax.ppermute(value, "mem", [(0, 1), (3, 2)])

    def across(value):
        return lax.ppermute(value, "mem", [(1, 2), (2, 1)])

    def far(value):
        return lax.ppermute(value, "mem", [(0, 2), (3, 1)])

    plan = make_plan(who, retrieved[0], units_dev, CHUNKS[0])
    keys = memory_keys.reshape(units_dev, -1, width)
    values = memory_values.reshape(units_dev, -1, width)
    unit_tokens = memory_keys.shape[1]
    own, first = [], 0
    for count in PIECES:
        own.append(gather(plan, keys, values, unit_tokens, first, count))
        first += count
    ends = [inward(piece) for piece in own]
    own_t = jnp.transpose(queries, (1, 3, 2, 0)).reshape(heads, width, group_size * tokens)
    end_t = inward(own_t)

    tile = jnp.stack(
        [jnp.transpose(new_keys[0], (1, 0, 2)), jnp.transpose(new_values[0], (1, 2, 0))], axis=1
    )
    cur = jnp.stack([tile, inward(tile), across(tile), far(tile)])
    prior = lax.ppermute(cur, "span", [(at, at + 1) for at in range(lax.axis_size("span") - 1)])

    arrived = [across(own[0])]
    first = CHUNKS[0]
    for count in CHUNKS[1:]:
        arrived.append(across(pack(plan, own, ends, first, count)))
        first += count

    state = attend_new(scale, who, cur, prior, own_t, end_t)
    one = [(OWN, 0, own[0]), (OWN, PIECES[0], own[1]), (OWN, PIECES[0] + PIECES[1], own[2]), (RECV, 0, arrived[0])]
    state = attend_units(scale, who, plan, own_t, end_t, one, state, False, tokens)
    two = [(END, 0, ends[0]), (END, PIECES[0], ends[1]), (RECV, CHUNKS[0], arrived[1])]
    state = attend_units(scale, who, plan, own_t, end_t, two, state, False, tokens)
    three = [(END, PIECES[0] + PIECES[1], ends[2]), (RECV, CHUNKS[0] + CHUNKS[1], arrived[2])]
    out_own, out_end = attend_units(scale, who, plan, own_t, end_t, three, state, True, tokens)

    returned = lax.ppermute(out_end, "mem", [(1, 0), (2, 3)])
    rows = jnp.where(is_mid == 1, out_own, returned)
    moved = lax.all_to_all(rows, "head", split_axis=0, concat_axis=1, tiled=True)
    return moved[None]


def shifted(value, axis, steps):
    count = lax.axis_size(axis)
    first, last = (max(0, -steps), min(count, count - steps))
    return lax.ppermute(value, axis, [(source, source + steps) for source in range(first, last)])


def any_line(query, new_keys, new_values, memory_keys, memory_values, retrieved):
    queries = query[0]
    row_count, head_count, group_size, head_width = queries.shape
    score_scale = 1.0 / math.sqrt(head_width)
    mem_index = lax.axis_index("mem")
    block_index = lax.axis_index("span")
    row_position = mem_index * row_count + jnp.arange(row_count, dtype=jnp.int32)

    def update(carry_state, key_pair, key_mask):
        old_peak, old_total, old_accum = carry_state
        scores = (
            jnp.einsum("rhgd,khd->rhgk", queries, key_pair[0], preferred_element_type=jnp.float32)
            * score_scale
        )
        scores = jnp.where(key_mask, scores, NEG)
        new_peak = jnp.maximum(old_peak, jnp.max(scores, axis=-1))
        weights = jnp.where(key_mask, jnp.exp(scores - new_peak[..., None]), 0.0)
        factor = jnp.exp(old_peak - new_peak)
        new_total = old_total * factor + jnp.sum(weights, axis=-1)
        new_accum = old_accum * factor[..., None] + jnp.einsum(
            "rhgk,khd->rhgd",
            weights.astype(jnp.bfloat16),
            key_pair[1],
            preferred_element_type=jnp.float32,
        )
        return (new_peak, new_total, new_accum)

    def sweep(carry_state, key_pair, first_key, mask_maker):
        key_count = key_pair.shape[1]
        step_size = key_count if key_count <= 1024 else math.gcd(key_count, 512)

        def advance(step_index, loop_state):
            sub_pair = lax.dynamic_slice_in_dim(key_pair, step_index * step_size, step_size, 1)
            key_position = (
                first_key + step_index * step_size + jnp.arange(step_size, dtype=jnp.int32)
            )
            return update(loop_state, sub_pair, mask_maker(key_position))

        return lax.fori_loop(0, key_count // step_size, advance, carry_state)

    def current_mask(key_position):
        return (key_position[None, :] <= row_position[:, None])[:, None, None, :]

    def prior_mask(key_position):
        return ((key_position[None, :] > row_position[:, None]) & (block_index > 0))[
            :, None, None, :
        ]

    def full_mask(key_position):
        return jnp.ones((1, 1, 1, key_position.shape[0]), bool)

    carry_state = (
        jnp.full((row_count, head_count, group_size), NEG, jnp.float32),
        jnp.zeros((row_count, head_count, group_size), jnp.float32),
        jnp.zeros((row_count, head_count, group_size, head_width), jnp.float32),
    )
    own_pair = jnp.stack([new_keys[0], new_values[0]])
    prior_pair = shifted(own_pair, "span", 1)
    loop_state = carry_state
    first_key = jnp.int32(0)
    loop_state = sweep(
        loop_state, lax.all_gather(own_pair, "mem", axis=1, tiled=True), first_key, current_mask
    )
    carry_state = sweep(
        loop_state, lax.all_gather(prior_pair, "mem", axis=1, tiled=True), first_key, prior_mask
    )
    unit_lists = retrieved[0]
    units_dev = memory_keys.shape[0]
    owners = unit_lists // units_dev
    local_units = unit_lists % units_dev
    owned_here = owners == mem_index
    gathered_pair = []
    for source_array in (memory_keys, memory_values):
        per_head = [
            source_array[local_units[head_at], :, head_at, :] for head_at in range(head_count)
        ]
        gathered_pair.append(jnp.stack(per_head, axis=2))
    gathered_units = jnp.stack(gathered_pair)
    keep_mask = jnp.transpose(owned_here)[None, :, None, :, None]
    slot_terms = jnp.where(keep_mask, gathered_units, jnp.zeros((), jnp.bfloat16))
    slot_terms = slot_terms.reshape(2, -1, head_count, head_width)
    summed_pair = lax.psum(slot_terms, "mem").astype(jnp.float32).astype(jnp.bfloat16)
    carry_state = sweep(carry_state, summed_pair, 0, full_mask)
    final_peak, final_total, final_accum = carry_state
    attended = (final_accum / final_total[..., None]).astype(jnp.bfloat16)
    attended = attended.reshape(row_count, head_count * group_size * head_width)
    moved = lax.all_to_all(attended, "head", split_axis=0, concat_axis=1, tiled=True)
    return moved[None]


def solution(mesh):
    local = line_of_four if mesh.shape["mem"] == 4 and mesh.shape["head"] == 2 else any_line
    return jax.shard_map(
        local,
        mesh=mesh,
        in_specs=(
            P("span", "mem", "head", None, None),
            P("span", "mem", "head", None),
            P("span", "mem", "head", None),
            P("mem", None, "head", None),
            P("mem", None, "head", None),
            P("span", "head", None),
        ),
        out_specs=P("span", ("mem", "head"), None),
        check_vma=False,
    )
```

```python
import functools
import math

import jax
import jax.numpy as jnp
from jax import lax
from jax.experimental import pallas as pl
from jax.experimental.pallas import tpu as pltpu
from jax.sharding import PartitionSpec as P

NEG = -1e30
LANES = 128
VMEM = 56 * 1024 * 1024
TINY = pl.CostEstimate(flops=1000, bytes_accessed=1000, transcendentals=0)
AHEAD = 6

PIECES = (16, 16)
CHUNKS = (16, 16, 16)
FIRST = 16
TILE = 4

ME, ENDER, OPPOSITE, FAR, LOW, PRIOR, MIDDLE, GROUP = range(8)
OWN, END, STREAM, EXTRA = range(4)


def smem():
    return pl.BlockSpec(memory_space=pltpu.SMEM)


def vmem():
    return pl.BlockSpec(memory_space=pltpu.VMEM)


def hbm():
    return pl.BlockSpec(memory_space=pl.ANY)


def head_picker(tokens, rows, head):
    token = lax.broadcasted_iota(jnp.int32, (tokens, rows), 0)
    row = lax.broadcasted_iota(jnp.int32, (tokens, rows), 1)
    return (row == token * (rows // tokens) + head).astype(jnp.bfloat16)


def pick_pair(pick, keys, values):
    keys = jnp.dot(pick, keys, preferred_element_type=jnp.float32)
    values_t = lax.dot_general(
        values, pick, (((0,), (1,)), ((), ())), preferred_element_type=jnp.float32
    )
    return keys.astype(jnp.bfloat16), values_t.astype(jnp.bfloat16)


def plan_units(units_dev, who_ref, list_ref, count_ref, table_ref):
    heads, topk = list_ref.shape
    me = who_ref[ME]

    def clear(at, _):
        count_ref[at] = 0
        return 0

    lax.fori_loop(0, count_ref.shape[0], clear, 0)
    used = jnp.int32(0)
    for head in range(heads):

        def note(at, used, head=head):
            unit = list_ref[head, at]
            owner = lax.div(unit, jnp.int32(units_dev))
            entry = owner * heads + head
            count_ref[entry] = count_ref[entry] + 1
            table_ref[used] = (unit - owner * units_dev) * heads + head
            return used + (owner == me).astype(jnp.int32)

        used = lax.fori_loop(0, topk, note, used)
    table_ref[heads * topk] = used


def gather_kernel(units_dev, pieces, first, tile, who_ref, list_ref, keys_ref, values_ref, *refs):
    refs = list(refs)
    heads, topk = list_ref.shape
    if tile:
        new_keys, new_values, count_ref, table_ref = (refs.pop(0) for _ in range(4))
        plan_units(units_dev, who_ref, list_ref, count_ref, table_ref)
    else:
        table_ref = refs.pop(0)
    outs = [refs.pop(0) for _ in pieces]
    key_buf, value_buf, picks, sems = refs
    rows = keys_ref.shape[1]
    tokens = rows // heads
    used = table_ref[heads * topk]

    def copies(at):
        unit = lax.div(table_ref[at], jnp.int32(heads))
        slot = lax.rem(at, jnp.int32(AHEAD))
        return (
            pltpu.make_async_copy(keys_ref.at[unit], key_buf.at[slot], sems.at[slot, 0]),
            pltpu.make_async_copy(values_ref.at[unit], value_buf.at[slot], sems.at[slot, 1]),
        )

    def start(at, _):
        for copy in copies(at):
            copy.start()
        return 0

    stop = jnp.minimum(used, first + sum(pieces))
    lax.fori_loop(first, jnp.minimum(stop, first + AHEAD), start, 0)
    for head in range(heads):
        picks[head] = head_picker(tokens, rows, head)
    base, place = first, TILE if tile else 0
    if tile:
        for head in range(heads):
            outs[0][head, 0], outs[0][head, 1] = pick_pair(picks[head], new_keys[...], new_values[...])
    for out_ref, size in zip(outs, pieces):

        def item(slot, _, out_ref=out_ref, base=base, place=place):
            at = base + slot
            for copy in copies(at):
                copy.wait()
            here = lax.rem(at, jnp.int32(AHEAD))
            pick = picks[lax.rem(table_ref[at], jnp.int32(heads))]
            out_ref[place + slot, 0], out_ref[place + slot, 1] = pick_pair(
                pick, key_buf[here], value_buf[here]
            )

            @pl.when(at + AHEAD < stop)
            def _():
                start(at + AHEAD, 0)

            return 0

        lax.fori_loop(0, jnp.clip(used - base, 0, size), item, 0)
        base, place = base + size, 0


def gather(who, unit_lists, keys, values, pieces, first, tile=None, table=None, n_owner=None):
    units, rows, width = keys.shape
    heads, topk = unit_lists.shape
    tokens = rows // heads
    extra = [TILE if tile is not None else 0] + [0] * (len(pieces) - 1)
    tables = [
        jax.ShapeDtypeStruct((size,), jnp.int32)
        for size in ([n_owner * heads, heads * topk + 1] if tile is not None else [])
    ]
    return pl.pallas_call(
        functools.partial(gather_kernel, units, pieces, first, tile is not None),
        out_shape=tuple(
            tables
            + [
                jax.ShapeDtypeStruct((size + more, 2, tokens, width), jnp.bfloat16)
                for size, more in zip(pieces, extra)
            ]
        ),
        in_specs=[smem(), smem(), hbm(), hbm()] + ([vmem()] * 2 if tile is not None else [smem()]),
        out_specs=tuple([smem()] * len(tables) + [vmem()] * len(pieces)),
        scratch_shapes=[
            pltpu.VMEM((AHEAD, rows, width), jnp.bfloat16),
            pltpu.VMEM((AHEAD, rows, width), jnp.bfloat16),
            pltpu.VMEM((heads, tokens, rows), jnp.bfloat16),
            pltpu.SemaphoreType.DMA((AHEAD, 2)),
        ],
        compiler_params=pltpu.CompilerParams(vmem_limit_bytes=VMEM),
        cost_estimate=TINY,
    )(who, unit_lists, keys, values, *(tile if tile is not None else (table,)))


def head_ranges(count_ref, heads, owner):
    ranges, at = [], jnp.int32(0)
    for head in range(heads):
        after = at + count_ref[owner * heads + head]
        ranges.append((at, after))
        at = after
    return ranges, at


def stream_shape(chunks, n_middle, n_end):
    extra = jnp.maximum(n_middle + n_end - sum(chunks), 0)
    return extra, jnp.maximum(n_middle - extra, FIRST)


def pack_kernel(heads, chunks, first, layout, who_ref, count_ref, *refs):
    sources = refs[: len(layout)]
    out_ref, sems = refs[len(layout) :]
    size = out_ref.shape[0]

    @pl.when(who_ref[MIDDLE] == 1)
    def _():
        _, n_own = head_ranges(count_ref, heads, who_ref[ME])
        _, n_end = head_ranges(count_ref, heads, who_ref[ENDER])
        extra, base = stream_shape(chunks, n_own, n_end)

        def each(act):
            for (kind, at, skip), ref in zip(layout, sources):
                shift, total = (-extra, n_own) if kind == OWN else (base, n_end)
                count = ref.shape[0] - skip
                low = jnp.maximum(at + shift, first)
                high = jnp.minimum(jnp.minimum(at + count, total) + shift, first + size)

                def one(slot, _, ref=ref, shift=shift, at=at, skip=skip):
                    place = slot - first
                    act(
                        pltpu.make_async_copy(
                            ref.at[slot - shift - at + skip], out_ref.at[place], sems.at[place]
                        )
                    )
                    return 0

                lax.fori_loop(low, jnp.maximum(low, high), one, 0)

        each(lambda copy: copy.start())
        each(lambda copy: copy.wait())


def pack(who, counts, heads, chunks, first, size, sources):
    layout = tuple(source[:3] for source in sources)
    arrays = [source[3] for source in sources]
    return pl.pallas_call(
        functools.partial(pack_kernel, heads, chunks, first, layout),
        out_shape=jax.ShapeDtypeStruct((size,) + arrays[0].shape[1:], jnp.bfloat16),
        in_specs=[smem(), smem()] + [hbm()] * len(arrays),
        out_specs=vmem(),
        scratch_shapes=[pltpu.SemaphoreType.DMA((size,))],
        compiler_params=pltpu.CompilerParams(vmem_limit_bytes=VMEM),
        cost_estimate=TINY,
    )(who, counts, *arrays)


def attend(scale, keys, values_t, queries_t, mask, state):
    peak, total, accum = state
    scores = jnp.dot(keys, queries_t, preferred_element_type=jnp.float32)
    if mask is not None:
        scores = jnp.where(mask, scores, NEG)
    new_peak = jnp.maximum(peak, jnp.max(scores, axis=0, keepdims=True))
    weights = jnp.exp2((scores - new_peak) * scale)
    factor = jnp.exp2((peak - new_peak) * scale)
    total = total * factor + jnp.sum(weights, axis=0, keepdims=True)
    accum = accum * factor + jnp.dot(
        values_t, weights.astype(jnp.bfloat16), preferred_element_type=jnp.float32
    )
    return new_peak, total, accum


def attend_kernel(scale, chunks, layout, n_query, parts, n_state, last, *refs):
    new = any(part[3] for part in parts)
    refs = list(refs)
    who_ref, count_ref = refs.pop(0), refs.pop(0)
    query_in = [refs.pop(0) for _ in range(n_query)]
    buffers = [refs.pop(0) for _ in layout]
    if new:
        cur_own, cur_rest, prior = (refs.pop(0) for _ in range(3))
    state_in = [refs.pop(0) for _ in range(n_state)]
    outs = [refs.pop(0) for _ in range(4 if last else 3)]
    queries, peak_ref, total_ref, accum_ref, units, unit_sems, state_sems, query_sems = refs
    state_refs = (peak_ref, total_ref, accum_ref)
    n_turn, width, rows = queries.shape
    tokens = units.shape[2]
    heads = list(count_ref.shape)[0] // 4

    def update(turn, keys, values_t, mask=None):
        for start in range(0, rows, LANES):
            lanes = pl.ds(start, LANES)
            state = tuple(ref[turn, :, lanes] for ref in state_refs)
            state = attend(scale, keys, values_t, queries[turn, :, lanes], mask, state)
            for ref, part in zip(state_refs, state):
                ref[turn, :, lanes] = part

    def new_tiles(turn, head, group):
        low, has_prior = who_ref[LOW] == 1, who_ref[PRIOR] == 1

        def tile(ref, at=0):
            return ref[at * TILE + head, 0], ref[at * TILE + head, 1]

        def choose(flag, yes, no):
            return tuple(jnp.where(flag, a, b) for a, b in zip(yes, no))

        def join(a, b):
            return jnp.concatenate([a[0], b[0]], axis=0), jnp.concatenate([a[1], b[1]], axis=1)

        key = lax.broadcasted_iota(jnp.int32, (2 * tokens, LANES), 0)
        position = lax.broadcasted_iota(jnp.int32, (2 * tokens, LANES), 1) % tokens
        mask = ((key < tokens) & (key <= position)) | (
            (key >= tokens) & (key - tokens > position) & has_prior
        )

        def both():
            pairs = [choose(low, tile(prior, at + 1), tile(cur_rest, at)) for at in (1, 2)]
            update(turn, *join(*pairs))

        if group == 0:
            update(turn, *join(tile(cur_own), tile(prior)), mask)

            @pl.when(low | has_prior)
            def _():
                update(turn, *choose(low, tile(cur_rest), tile(prior, 1)))

            pl.when(jnp.logical_not(low) | has_prior)(both)
        else:
            update(turn, *join(tile(cur_rest), tile(prior, 1)), mask)

            @pl.when(jnp.logical_not(low) | has_prior)
            def _():
                update(turn, *choose(low, tile(prior), tile(cur_own)))
                both()

    @pl.when(who_ref[MIDDLE] == 1)
    def _():
        loads = []
        at = parts[0][0]
        for number, ref in enumerate(query_in):
            here = pl.ds(at, ref.shape[0])
            loads.append(pltpu.make_async_copy(ref, queries.at[here], query_sems.at[number]))
            at += ref.shape[0]
        for number, (lowest, highest, _, _, fresh) in enumerate(parts):
            if not fresh:
                here = pl.ds(lowest, highest - lowest)
                loads += [
                    pltpu.make_async_copy(source.at[here], ref.at[here], state_sems.at[number, at])
                    for at, (source, ref) in enumerate(zip(state_in, state_refs))
                ]
        for load in loads:
            load.start()

        ranges, totals = zip(
            *(head_ranges(count_ref, heads, who_ref[role]) for role in (ME, ENDER, OPPOSITE, FAR))
        )
        extra, base = stream_shape(chunks, totals[2], totals[3])
        n_stage = max(entry[3] for entry in layout) + 1
        place, bounds = jnp.int32(0), []
        for head in range(heads):
            stage_at = -1
            for (kind, first, skip, stage), buffer in zip(layout, buffers):
                while stage_at < stage:
                    stage_at += 1
                    bounds.append(place)
                if kind == STREAM:
                    low, high = ranges[2][head]
                    spans = [
                        (low, jnp.minimum(high, FIRST)),
                        (jnp.maximum(low, FIRST + extra) - extra, high - extra),
                    ]
                    low, high = ranges[3][head]
                    spans.append((base + low, base + high))
                elif kind == EXTRA:
                    low, high = ranges[2][head]
                    spans = [(jnp.maximum(low, FIRST), jnp.minimum(high, FIRST + extra))]
                else:
                    spans = [ranges[0 if kind == OWN else 1][head]]
                for low, high in spans:
                    low = jnp.maximum(low - first, 0)
                    high = jnp.maximum(jnp.minimum(high - first, buffer.shape[0] - skip), low)

                    def fetch(at, _, buffer=buffer, skip=skip, shift=place - low):
                        slot = at + shift
                        pltpu.make_async_copy(
                            buffer.at[at + skip], units.at[slot], unit_sems.at[slot]
                        ).start()
                        return 0

                    lax.fori_loop(low, high, fetch, 0)
                    place = place + high - low
            bounds.append(place)

        def arrived(slot, _):
            pltpu.make_async_copy(buffers[0].at[0], units.at[slot], unit_sems.at[slot]).wait()
            return 0

        lax.fori_loop(0, place, arrived, 0)
        for load in loads:
            load.wait()

        def one_turn(turn, _, group, stage, tiles, fresh):
            head = lax.rem(turn, jnp.int32(heads))
            if fresh:
                peak_ref[turn] = jnp.full((1, rows), NEG, jnp.float32)
                total_ref[turn] = jnp.zeros((1, rows), jnp.float32)
                accum_ref[turn] = jnp.zeros((width, rows), jnp.float32)
            if tiles:
                new_tiles(turn, head, group)
            low, high = jnp.int32(0), jnp.int32(0)
            for at in range(heads):
                low = jnp.where(head == at, bounds[at * (n_stage + 1) + stage], low)
                high = jnp.where(head == at, bounds[at * (n_stage + 1) + n_stage], high)

            def several(slot, count):
                keys = units[pl.ds(slot, count), 0].reshape(count * tokens, width)
                values_t = jnp.concatenate([units[slot + at, 1] for at in range(count)], axis=1)
                update(turn, keys, values_t)

            fours = lax.div(high - low, jnp.int32(4))

            def four(at, _):
                several(low + 4 * at, 4)
                return 0

            lax.fori_loop(0, fours, four, 0)
            left = high - low - 4 * fours

            @pl.when(left >= 2)
            def _():
                several(high - left, 2)

            @pl.when((left == 1) | (left == 3))
            def _():
                several(high - 1, 1)

            if last:
                keep_own, send_own, keep_end, send_end = outs
                half = tokens // 2
                first_group = who_ref[GROUP] == 0
                for own_rows, keep_ref, send_ref in (
                    (True, keep_own, send_own),
                    (False, keep_end, send_end),
                ):

                    @pl.when((turn < heads) == own_rows)
                    def _(keep_ref=keep_ref, send_ref=send_ref):
                        for member in range(rows // tokens):
                            lanes = pl.ds(member * tokens, tokens)
                            result = accum_ref[turn, :, lanes] / total_ref[turn, :, lanes]
                            result = result.T
                            top, bottom = result[:half], result[half:]
                            column = pl.ds(
                                pl.multiple_of((head * (rows // tokens) + member) * width, width), width
                            )
                            keep_ref[:, column] = jnp.where(first_group, top, bottom).astype(jnp.bfloat16)
                            send_ref[:, column] = jnp.where(first_group, bottom, top).astype(jnp.bfloat16)

            return 0

        for lowest, highest, stage, tiles, fresh in parts:
            body = functools.partial(
                one_turn, group=0 if lowest < heads else 1, stage=stage, tiles=tiles, fresh=fresh
            )
            lax.fori_loop(lowest, highest, body, 0)
        if not last:
            stores = []
            for number, (lowest, highest, _, _, _) in enumerate(parts):
                here = pl.ds(lowest, highest - lowest)
                stores += [
                    pltpu.make_async_copy(ref.at[here], out.at[here], state_sems.at[number, at])
                    for at, (ref, out) in enumerate(zip(state_refs, outs))
                ]
            for store in stores:
                store.start()
            for store in stores:
                store.wait()


def attend_call(scale, chunks, who, counts, tokens, parts, queries, buffers, state, tiles=None, last=False):
    layout = tuple(buffer[:3] + (buffer[4],) for buffer in buffers)
    arrays = [buffer[3] for buffer in buffers]
    _, width, rows = queries[0].shape
    n_turn = 2 * (counts.shape[0] // 4)
    heads = counts.shape[0] // 4
    n_units = sum(array.shape[0] - buffer[2] for array, buffer in zip(arrays, buffers))
    state_shapes = [(n_turn, 1, rows), (n_turn, 1, rows), (n_turn, width, rows)]
    if last:
        outs = [jax.ShapeDtypeStruct((tokens // 2, heads * (rows // tokens) * width), jnp.bfloat16)] * 4
    else:
        outs = [jax.ShapeDtypeStruct(shape, jnp.float32) for shape in state_shapes]
    given = [] if state is None else list(state)
    tile_args = [] if tiles is None else list(tiles)
    before = 2 + len(queries) + len(arrays) + len(tile_args)
    aliases = {} if last or state is None else {before + at: at for at in range(3)}
    return pl.pallas_call(
        functools.partial(
            attend_kernel,
            scale,
            chunks,
            layout,
            len(queries),
            tuple(parts),
            len(given),
            last,
        ),
        out_shape=tuple(outs),
        in_specs=[smem(), smem()]
        + [hbm()] * (len(queries) + len(arrays))
        + [vmem()] * len(tile_args)
        + [hbm()] * len(given),
        out_specs=tuple([vmem() if last else hbm()] * len(outs)),
        scratch_shapes=[pltpu.VMEM((n_turn, width, rows), jnp.bfloat16)]
        + [pltpu.VMEM(shape, jnp.float32) for shape in state_shapes]
        + [
            pltpu.VMEM((n_units,) + arrays[0].shape[1:], jnp.bfloat16),
            pltpu.SemaphoreType.DMA((n_units,)),
            pltpu.SemaphoreType.DMA((len(parts), 3)),
            pltpu.SemaphoreType.DMA((len(queries),)),
        ],
        input_output_aliases=aliases,
        compiler_params=pltpu.CompilerParams(vmem_limit_bytes=VMEM),
        cost_estimate=TINY,
    )(who, counts, *queries, *arrays, *tile_args, *given)


def line_of_four(query, new_keys, new_values, memory_keys, memory_values, retrieved):
    queries = query[0]
    tokens, heads, group_size, width = queries.shape
    units_dev = memory_keys.shape[0]
    scale = math.log2(math.e) / math.sqrt(width)
    me = lax.axis_index("mem")
    span = lax.axis_index("span")
    group = lax.axis_index("head")
    low = (me < 2).astype(jnp.int32)
    middle = (me == 1) | (me == 2)
    end = jnp.where(low == 1, 0, 3)
    who = jnp.stack([me, end, 3 - me, 3 - end, low, span > 0, middle, group]).astype(jnp.int32)

    def inward(value):
        return lax.ppermute(value, "mem", [(0, 1), (3, 2)])

    def across(value):
        return lax.ppermute(value, "mem", [(1, 2), (2, 1)])

    def far(value):
        return lax.ppermute(value, "mem", [(0, 2), (3, 1)])

    def onward(value):
        return lax.ppermute(value, "span", [(at, at + 1) for at in range(lax.axis_size("span") - 1)])

    n_mem = lax.axis_size("mem")

    def after(value, before):
        return lax.optimization_barrier((value, before))[0]

    own_t = jnp.transpose(queries, (1, 3, 2, 0)).reshape(heads, width, group_size * tokens)
    end_t = inward(own_t)
    keys = memory_keys.reshape(units_dev, -1, width)
    values = memory_values.reshape(units_dev, -1, width)
    tile_pair = (new_keys[0].reshape(-1, width), new_values[0].reshape(-1, width))
    unit_lists = after(retrieved[0], own_t)
    counts, table, own_0 = gather(who, unit_lists, keys, values, PIECES[:1], 0, tile=tile_pair, n_owner=n_mem)
    stream_0, end_0 = across(own_0), inward(after(own_0, end_t))
    tile = own_0[:TILE]
    far_tile = far(after(tile, stream_0))
    (own_1,) = gather(who, unit_lists, keys, values, PIECES[1:], PIECES[0], table=table)
    end_1 = inward(after(own_1, end_0))

    places = [sum(PIECES[:at]) for at in range(len(PIECES))]
    starts = [sum(CHUNKS[:at]) for at in range(len(CHUNKS))]
    own = [(OWN, places[0], TILE, own_0), (OWN, places[1], 0, own_1)]
    ends = [(END, places[0], TILE, end_0), (END, places[1], 0, end_1)]
    streams = [(STREAM, starts[0], TILE, stream_0)]
    call = functools.partial(attend_call, scale, CHUNKS, who, counts, tokens)

    def send_chunk(at, sources, state):
        sources = [source[:3] + (after(source[3], state[0]),) for source in sources]
        packed = pack(who, counts, heads, CHUNKS, starts[at], CHUNKS[at], sources)
        streams.append((STREAM, starts[at], 0, across(packed)))
        return [after(state[0], packed), *state[1:]]

    def stage(buffers, before=None):
        if before is not None:
            buffers = [buffer[:3] + (after(buffer[3], before[0]),) for buffer in buffers]
        return [buffer + (0,) for buffer in buffers]

    def parts(tiles, fresh):
        return [(0, heads, 0, tiles, fresh), (heads, 2 * heads, 0, tiles, fresh)]

    both_t = [own_t, end_t]
    state = list(call(parts(False, True), both_t, stage(own + streams), None))
    state = send_chunk(1, own[1:] + ends[:1], state)
    rest = jnp.concatenate([after(part, state[0])[:TILE] for part in (end_0, stream_0, far_tile)])
    tiles = (tile, rest, onward(jnp.concatenate([tile, rest])))
    state = list(call(parts(False, False), both_t, stage(ends[:1], state), state))
    state = send_chunk(2, own[1:] + ends, state)
    state = list(call(parts(True, False), both_t, stage(ends[1:] + streams[1:2], state), state, tiles=tiles))
    last_streams = stage(streams[2:], state)
    final = functools.partial(call, parts(False, False), both_t, last=True)

    def fits(piece, state):
        return final(last_streams, state)

    def exceeds(piece, state):
        return final(last_streams + [(EXTRA, places[-1], 0, across(piece), 0)], state)

    by_owner = counts.reshape(-1, heads).sum(axis=1)
    over = jnp.maximum(by_owner[0] + by_owner[1], by_owner[2] + by_owner[3]) > sum(CHUNKS)
    keep_own, send_own, keep_end, send_end = lax.cond(over, exceeds, fits, own_1, tuple(state))

    n_head = lax.axis_size("head")

    def pairs(moves):
        return [
            (source * n_head + at, target * n_head + (at + turn) % n_head)
            for source, target, turn in moves
            for at in range(n_head)
        ]

    axes = ("mem", "head")
    kept = lax.ppermute(keep_end, axes, pairs([(1, 0, 0), (2, 3, 0)]))
    swapped_end = lax.ppermute(send_end, axes, pairs([(1, 0, 1), (2, 3, 1)]))
    swapped_own = lax.ppermute(send_own, axes, pairs([(1, 1, 1), (2, 2, 1)]))
    same = jnp.where(middle, keep_own, kept)
    other = jnp.where(middle, swapped_own, swapped_end)
    left = jnp.where(group == 0, same, other)
    right = jnp.where(group == 0, other, same)
    return jnp.concatenate([left, right], axis=1)[None]


def shifted(value, axis, steps):
    count = lax.axis_size(axis)
    first, last = (max(0, -steps), min(count, count - steps))
    return lax.ppermute(value, axis, [(source, source + steps) for source in range(first, last)])


def any_line(query, new_keys, new_values, memory_keys, memory_values, retrieved):
    queries = query[0]
    row_count, head_count, group_size, head_width = queries.shape
    score_scale = 1.0 / math.sqrt(head_width)
    mem_index = lax.axis_index("mem")
    block_index = lax.axis_index("span")
    row_position = mem_index * row_count + jnp.arange(row_count, dtype=jnp.int32)

    def update(carry_state, key_pair, key_mask):
        old_peak, old_total, old_accum = carry_state
        scores = (
            jnp.einsum("rhgd,khd->rhgk", queries, key_pair[0], preferred_element_type=jnp.float32)
            * score_scale
        )
        scores = jnp.where(key_mask, scores, NEG)
        new_peak = jnp.maximum(old_peak, jnp.max(scores, axis=-1))
        weights = jnp.where(key_mask, jnp.exp(scores - new_peak[..., None]), 0.0)
        factor = jnp.exp(old_peak - new_peak)
        new_total = old_total * factor + jnp.sum(weights, axis=-1)
        new_accum = old_accum * factor[..., None] + jnp.einsum(
            "rhgk,khd->rhgd",
            weights.astype(jnp.bfloat16),
            key_pair[1],
            preferred_element_type=jnp.float32,
        )
        return (new_peak, new_total, new_accum)

    def sweep(carry_state, key_pair, first_key, mask_maker):
        key_count = key_pair.shape[1]
        step_size = key_count if key_count <= 1024 else math.gcd(key_count, 512)

        def advance(step_index, loop_state):
            sub_pair = lax.dynamic_slice_in_dim(key_pair, step_index * step_size, step_size, 1)
            key_position = (
                first_key + step_index * step_size + jnp.arange(step_size, dtype=jnp.int32)
            )
            return update(loop_state, sub_pair, mask_maker(key_position))

        return lax.fori_loop(0, key_count // step_size, advance, carry_state)

    def current_mask(key_position):
        return (key_position[None, :] <= row_position[:, None])[:, None, None, :]

    def prior_mask(key_position):
        return ((key_position[None, :] > row_position[:, None]) & (block_index > 0))[
            :, None, None, :
        ]

    def full_mask(key_position):
        return jnp.ones((1, 1, 1, key_position.shape[0]), bool)

    carry_state = (
        jnp.full((row_count, head_count, group_size), NEG, jnp.float32),
        jnp.zeros((row_count, head_count, group_size), jnp.float32),
        jnp.zeros((row_count, head_count, group_size, head_width), jnp.float32),
    )
    own_pair = jnp.stack([new_keys[0], new_values[0]])
    prior_pair = shifted(own_pair, "span", 1)
    loop_state = carry_state
    first_key = jnp.int32(0)
    loop_state = sweep(
        loop_state, lax.all_gather(own_pair, "mem", axis=1, tiled=True), first_key, current_mask
    )
    carry_state = sweep(
        loop_state, lax.all_gather(prior_pair, "mem", axis=1, tiled=True), first_key, prior_mask
    )
    unit_lists = retrieved[0]
    units_dev = memory_keys.shape[0]
    owners = unit_lists // units_dev
    local_units = unit_lists % units_dev
    owned_here = owners == mem_index
    gathered_pair = []
    for source_array in (memory_keys, memory_values):
        per_head = [
            source_array[local_units[head_at], :, head_at, :] for head_at in range(head_count)
        ]
        gathered_pair.append(jnp.stack(per_head, axis=2))
    gathered_units = jnp.stack(gathered_pair)
    keep_mask = jnp.transpose(owned_here)[None, :, None, :, None]
    slot_terms = jnp.where(keep_mask, gathered_units, jnp.zeros((), jnp.bfloat16))
    slot_terms = slot_terms.reshape(2, -1, head_count, head_width)
    summed_pair = lax.psum(slot_terms, "mem").astype(jnp.float32).astype(jnp.bfloat16)
    carry_state = sweep(carry_state, summed_pair, 0, full_mask)
    final_peak, final_total, final_accum = carry_state
    attended = (final_accum / final_total[..., None]).astype(jnp.bfloat16)
    attended = attended.reshape(row_count, head_count * group_size * head_width)
    moved = lax.all_to_all(attended, "head", split_axis=0, concat_axis=1, tiled=True)
    return moved[None]


def solution(mesh):
    local = line_of_four if mesh.shape["mem"] == 4 and mesh.shape["head"] == 2 else any_line
    return jax.shard_map(
        local,
        mesh=mesh,
        in_specs=(
            P("span", "mem", "head", None, None),
            P("span", "mem", "head", None),
            P("span", "mem", "head", None),
            P("mem", None, "head", None),
            P("mem", None, "head", None),
            P("span", "head", None),
        ),
        out_specs=P("span", ("mem", "head"), None),
        check_vma=False,
    )
```

```python
import functools
import math

import jax
import jax.numpy as jnp
from jax import lax
from jax.experimental import pallas as pl
from jax.experimental.pallas import tpu as pltpu
from jax.sharding import PartitionSpec as P

NEG = -1e30
LANES = 128
VMEM = 56 * 1024 * 1024
TINY = pl.CostEstimate(flops=1000, bytes_accessed=1000, transcendentals=0)
AHEAD = 6

PIECES = (16, 16)
CHUNKS = (16, 16, 16)
FIRST = 16
TILE = 4

ME, ENDER, OPPOSITE, FAR, LOW, PRIOR, MIDDLE, GROUP = range(8)
OWN, END, STREAM, EXTRA = range(4)


def smem():
    return pl.BlockSpec(memory_space=pltpu.SMEM)


def vmem():
    return pl.BlockSpec(memory_space=pltpu.VMEM)


def hbm():
    return pl.BlockSpec(memory_space=pl.ANY)


def head_picker(tokens, rows, head):
    token = lax.broadcasted_iota(jnp.int32, (tokens, rows), 0)
    row = lax.broadcasted_iota(jnp.int32, (tokens, rows), 1)
    return (row == token * (rows // tokens) + head).astype(jnp.bfloat16)


def pick_pair(pick, keys, values):
    keys = jnp.dot(pick, keys, preferred_element_type=jnp.float32)
    values_t = lax.dot_general(
        values, pick, (((0,), (1,)), ((), ())), preferred_element_type=jnp.float32
    )
    return keys.astype(jnp.bfloat16), values_t.astype(jnp.bfloat16)


def plan_units(units_dev, who_ref, list_ref, count_ref, table_ref):
    heads, topk = list_ref.shape
    me = who_ref[ME]

    def clear(at, _):
        count_ref[at] = 0
        return 0

    lax.fori_loop(0, count_ref.shape[0], clear, 0)
    used = jnp.int32(0)
    for head in range(heads):

        def note(at, used, head=head):
            unit = list_ref[head, at]
            owner = lax.div(unit, jnp.int32(units_dev))
            entry = owner * heads + head
            count_ref[entry] = count_ref[entry] + 1
            table_ref[used] = (unit - owner * units_dev) * heads + head
            return used + (owner == me).astype(jnp.int32)

        used = lax.fori_loop(0, topk, note, used)
    table_ref[heads * topk] = used


def gather_kernel(units_dev, pieces, first, tile, who_ref, list_ref, keys_ref, values_ref, *refs):
    refs = list(refs)
    heads, topk = list_ref.shape
    if tile:
        new_keys, new_values, count_ref, table_ref = (refs.pop(0) for _ in range(4))
        plan_units(units_dev, who_ref, list_ref, count_ref, table_ref)
    else:
        table_ref = refs.pop(0)
    outs = [refs.pop(0) for _ in pieces]
    key_buf, value_buf, picks, sems = refs
    rows = keys_ref.shape[1]
    tokens = rows // heads
    used = table_ref[heads * topk]

    def copies(at):
        unit = lax.div(table_ref[at], jnp.int32(heads))
        slot = lax.rem(at, jnp.int32(AHEAD))
        return (
            pltpu.make_async_copy(keys_ref.at[unit], key_buf.at[slot], sems.at[slot, 0]),
            pltpu.make_async_copy(values_ref.at[unit], value_buf.at[slot], sems.at[slot, 1]),
        )

    def start(at, _):
        for copy in copies(at):
            copy.start()
        return 0

    stop = jnp.minimum(used, first + sum(pieces))
    lax.fori_loop(first, jnp.minimum(stop, first + AHEAD), start, 0)
    for head in range(heads):
        picks[head] = head_picker(tokens, rows, head)
    base, place = first, TILE if tile else 0
    if tile:
        for head in range(heads):
            outs[0][head, 0], outs[0][head, 1] = pick_pair(picks[head], new_keys[...], new_values[...])
    for out_ref, size in zip(outs, pieces):

        def item(slot, _, out_ref=out_ref, base=base, place=place):
            at = base + slot
            for copy in copies(at):
                copy.wait()
            here = lax.rem(at, jnp.int32(AHEAD))
            pick = picks[lax.rem(table_ref[at], jnp.int32(heads))]
            out_ref[place + slot, 0], out_ref[place + slot, 1] = pick_pair(
                pick, key_buf[here], value_buf[here]
            )

            @pl.when(at + AHEAD < stop)
            def _():
                start(at + AHEAD, 0)

            return 0

        lax.fori_loop(0, jnp.clip(used - base, 0, size), item, 0)
        base, place = base + size, 0


def gather(who, unit_lists, keys, values, pieces, first, tile=None, table=None, n_owner=None):
    units, rows, width = keys.shape
    heads, topk = unit_lists.shape
    tokens = rows // heads
    extra = [TILE if tile is not None else 0] + [0] * (len(pieces) - 1)
    tables = [
        jax.ShapeDtypeStruct((size,), jnp.int32)
        for size in ([n_owner * heads, heads * topk + 1] if tile is not None else [])
    ]
    return pl.pallas_call(
        functools.partial(gather_kernel, units, pieces, first, tile is not None),
        out_shape=tuple(
            tables
            + [
                jax.ShapeDtypeStruct((size + more, 2, tokens, width), jnp.bfloat16)
                for size, more in zip(pieces, extra)
            ]
        ),
        in_specs=[smem(), smem(), hbm(), hbm()] + ([vmem()] * 2 if tile is not None else [smem()]),
        out_specs=tuple([smem()] * len(tables) + [vmem()] * len(pieces)),
        scratch_shapes=[
            pltpu.VMEM((AHEAD, rows, width), jnp.bfloat16),
            pltpu.VMEM((AHEAD, rows, width), jnp.bfloat16),
            pltpu.VMEM((heads, tokens, rows), jnp.bfloat16),
            pltpu.SemaphoreType.DMA((AHEAD, 2)),
        ],
        compiler_params=pltpu.CompilerParams(vmem_limit_bytes=VMEM),
        cost_estimate=TINY,
    )(who, unit_lists, keys, values, *(tile if tile is not None else (table,)))


def head_ranges(count_ref, heads, owner):
    ranges, at = [], jnp.int32(0)
    for head in range(heads):
        after = at + count_ref[owner * heads + head]
        ranges.append((at, after))
        at = after
    return ranges, at


def stream_shape(chunks, n_middle, n_end):
    extra = jnp.maximum(n_middle + n_end - sum(chunks), 0)
    return extra, jnp.maximum(n_middle - extra, FIRST)


def pack_kernel(heads, chunks, first, layout, who_ref, count_ref, *refs):
    sources = refs[: len(layout)]
    out_ref, sems = refs[len(layout) :]
    size = out_ref.shape[0]

    @pl.when(who_ref[MIDDLE] == 1)
    def _():
        _, n_own = head_ranges(count_ref, heads, who_ref[ME])
        _, n_end = head_ranges(count_ref, heads, who_ref[ENDER])
        extra, base = stream_shape(chunks, n_own, n_end)

        def each(act):
            for (kind, at, skip), ref in zip(layout, sources):
                shift, total = (-extra, n_own) if kind == OWN else (base, n_end)
                count = ref.shape[0] - skip
                low = jnp.maximum(at + shift, first)
                high = jnp.minimum(jnp.minimum(at + count, total) + shift, first + size)

                def one(slot, _, ref=ref, shift=shift, at=at, skip=skip):
                    place = slot - first
                    act(
                        pltpu.make_async_copy(
                            ref.at[slot - shift - at + skip], out_ref.at[place], sems.at[place]
                        )
                    )
                    return 0

                lax.fori_loop(low, jnp.maximum(low, high), one, 0)

        each(lambda copy: copy.start())
        each(lambda copy: copy.wait())


def pack(who, counts, heads, chunks, first, size, sources):
    layout = tuple(source[:3] for source in sources)
    arrays = [source[3] for source in sources]
    return pl.pallas_call(
        functools.partial(pack_kernel, heads, chunks, first, layout),
        out_shape=jax.ShapeDtypeStruct((size,) + arrays[0].shape[1:], jnp.bfloat16),
        in_specs=[smem(), smem()] + [hbm()] * len(arrays),
        out_specs=vmem(),
        scratch_shapes=[pltpu.SemaphoreType.DMA((size,))],
        compiler_params=pltpu.CompilerParams(vmem_limit_bytes=VMEM),
        cost_estimate=TINY,
    )(who, counts, *arrays)


def attend(scale, keys, values_t, queries_t, mask, state):
    peak, total, accum = state
    scores = jnp.dot(keys, queries_t, preferred_element_type=jnp.float32)
    if mask is not None:
        scores = jnp.where(mask, scores, NEG)
    new_peak = jnp.maximum(peak, jnp.max(scores, axis=0, keepdims=True))
    weights = jnp.exp2((scores - new_peak) * scale)
    factor = jnp.exp2((peak - new_peak) * scale)
    total = total * factor + jnp.sum(weights, axis=0, keepdims=True)
    accum = accum * factor + jnp.dot(
        values_t, weights.astype(jnp.bfloat16), preferred_element_type=jnp.float32
    )
    return new_peak, total, accum


def attend_kernel(scale, chunks, layout, n_query, parts, n_state, last, *refs):
    new = any(part[3] for part in parts)
    refs = list(refs)
    who_ref, count_ref = refs.pop(0), refs.pop(0)
    query_in = [refs.pop(0) for _ in range(n_query)]
    buffers = [refs.pop(0) for _ in layout]
    if new:
        cur_own, cur_rest, prior = (refs.pop(0) for _ in range(3))
    state_in = [refs.pop(0) for _ in range(n_state)]
    outs = [refs.pop(0) for _ in range(4 if last else 3)]
    queries, peak_ref, total_ref, accum_ref, units, unit_sems, state_sems, query_sems = refs
    state_refs = (peak_ref, total_ref, accum_ref)
    n_turn, width, rows = queries.shape
    tokens = units.shape[2]
    heads = list(count_ref.shape)[0] // 4

    def update(turn, keys, values_t, mask=None):
        for start in range(0, rows, LANES):
            lanes = pl.ds(start, LANES)
            state = tuple(ref[turn, :, lanes] for ref in state_refs)
            state = attend(scale, keys, values_t, queries[turn, :, lanes], mask, state)
            for ref, part in zip(state_refs, state):
                ref[turn, :, lanes] = part

    def new_tiles(turn, head, group):
        low, has_prior = who_ref[LOW] == 1, who_ref[PRIOR] == 1

        def tile(ref, at=0):
            return ref[at * TILE + head, 0], ref[at * TILE + head, 1]

        def choose(flag, yes, no):
            return tuple(jnp.where(flag, a, b) for a, b in zip(yes, no))

        def join(a, b):
            return jnp.concatenate([a[0], b[0]], axis=0), jnp.concatenate([a[1], b[1]], axis=1)

        key = lax.broadcasted_iota(jnp.int32, (2 * tokens, LANES), 0)
        position = lax.broadcasted_iota(jnp.int32, (2 * tokens, LANES), 1) % tokens
        mask = ((key < tokens) & (key <= position)) | (
            (key >= tokens) & (key - tokens > position) & has_prior
        )

        def both():
            pairs = [choose(low, tile(prior, at + 1), tile(cur_rest, at)) for at in (1, 2)]
            update(turn, *join(*pairs))

        if group == 0:
            update(turn, *join(tile(cur_own), tile(prior)), mask)

            @pl.when(low | has_prior)
            def _():
                update(turn, *choose(low, tile(cur_rest), tile(prior, 1)))

            pl.when(jnp.logical_not(low) | has_prior)(both)
        else:
            update(turn, *join(tile(cur_rest), tile(prior, 1)), mask)

            @pl.when(jnp.logical_not(low) | has_prior)
            def _():
                update(turn, *choose(low, tile(prior), tile(cur_own)))
                both()

    @pl.when(who_ref[MIDDLE] == 1)
    def _():
        loads = []
        at = parts[0][0]
        for number, ref in enumerate(query_in):
            here = pl.ds(at, ref.shape[0])
            loads.append(pltpu.make_async_copy(ref, queries.at[here], query_sems.at[number]))
            at += ref.shape[0]
        for number, (lowest, highest, _, _, fresh) in enumerate(parts):
            if not fresh:
                here = pl.ds(lowest, highest - lowest)
                loads += [
                    pltpu.make_async_copy(source.at[here], ref.at[here], state_sems.at[number, at])
                    for at, (source, ref) in enumerate(zip(state_in, state_refs))
                ]
        for load in loads:
            load.start()

        ranges, totals = zip(
            *(head_ranges(count_ref, heads, who_ref[role]) for role in (ME, ENDER, OPPOSITE, FAR))
        )
        extra, base = stream_shape(chunks, totals[2], totals[3])
        n_stage = max(entry[3] for entry in layout) + 1
        place, bounds = jnp.int32(0), []
        for head in range(heads):
            stage_at = -1
            for (kind, first, skip, stage), buffer in zip(layout, buffers):
                while stage_at < stage:
                    stage_at += 1
                    bounds.append(place)
                if kind == STREAM:
                    low, high = ranges[2][head]
                    spans = [
                        (low, jnp.minimum(high, FIRST)),
                        (jnp.maximum(low, FIRST + extra) - extra, high - extra),
                    ]
                    low, high = ranges[3][head]
                    spans.append((base + low, base + high))
                elif kind == EXTRA:
                    low, high = ranges[2][head]
                    spans = [(jnp.maximum(low, FIRST), jnp.minimum(high, FIRST + extra))]
                else:
                    spans = [ranges[0 if kind == OWN else 1][head]]
                for low, high in spans:
                    low = jnp.maximum(low - first, 0)
                    high = jnp.maximum(jnp.minimum(high - first, buffer.shape[0] - skip), low)

                    def fetch(at, _, buffer=buffer, skip=skip, shift=place - low):
                        slot = at + shift
                        pltpu.make_async_copy(
                            buffer.at[at + skip], units.at[slot], unit_sems.at[slot]
                        ).start()
                        return 0

                    lax.fori_loop(low, high, fetch, 0)
                    place = place + high - low
            bounds.append(place)

        def arrived(slot, _):
            pltpu.make_async_copy(buffers[0].at[0], units.at[slot], unit_sems.at[slot]).wait()
            return 0

        lax.fori_loop(0, place, arrived, 0)
        for load in loads:
            load.wait()

        def one_turn(turn, _, group, stage, tiles, fresh):
            head = lax.rem(turn, jnp.int32(heads))
            if fresh:
                peak_ref[turn] = jnp.full((1, rows), NEG, jnp.float32)
                total_ref[turn] = jnp.zeros((1, rows), jnp.float32)
                accum_ref[turn] = jnp.zeros((width, rows), jnp.float32)
            if tiles:
                new_tiles(turn, head, group)
            low, high = jnp.int32(0), jnp.int32(0)
            for at in range(heads):
                low = jnp.where(head == at, bounds[at * (n_stage + 1) + stage], low)
                high = jnp.where(head == at, bounds[at * (n_stage + 1) + n_stage], high)

            def several(slot, count):
                keys = units[pl.ds(slot, count), 0].reshape(count * tokens, width)
                values_t = jnp.concatenate([units[slot + at, 1] for at in range(count)], axis=1)
                update(turn, keys, values_t)

            fours = lax.div(high - low, jnp.int32(4))

            def four(at, _):
                several(low + 4 * at, 4)
                return 0

            lax.fori_loop(0, fours, four, 0)
            left = high - low - 4 * fours

            @pl.when(left >= 2)
            def _():
                several(high - left, 2)

            @pl.when((left == 1) | (left == 3))
            def _():
                several(high - 1, 1)

            if last:
                keep_own, send_own, keep_end, send_end = outs
                half = tokens // 2
                first_group = who_ref[GROUP] == 0
                for own_rows, keep_ref, send_ref in (
                    (True, keep_own, send_own),
                    (False, keep_end, send_end),
                ):

                    @pl.when((turn < heads) == own_rows)
                    def _(keep_ref=keep_ref, send_ref=send_ref):
                        for member in range(rows // tokens):
                            lanes = pl.ds(member * tokens, tokens)
                            result = accum_ref[turn, :, lanes] / total_ref[turn, :, lanes]
                            result = result.T
                            top, bottom = result[:half], result[half:]
                            column = pl.ds(
                                pl.multiple_of((head * (rows // tokens) + member) * width, width), width
                            )
                            keep_ref[:, column] = jnp.where(first_group, top, bottom).astype(jnp.bfloat16)
                            send_ref[:, column] = jnp.where(first_group, bottom, top).astype(jnp.bfloat16)

            return 0

        for lowest, highest, stage, tiles, fresh in parts:
            body = functools.partial(
                one_turn, group=0 if lowest < heads else 1, stage=stage, tiles=tiles, fresh=fresh
            )
            lax.fori_loop(lowest, highest, body, 0)
        if not last:
            stores = []
            for number, (lowest, highest, _, _, _) in enumerate(parts):
                here = pl.ds(lowest, highest - lowest)
                stores += [
                    pltpu.make_async_copy(ref.at[here], out.at[here], state_sems.at[number, at])
                    for at, (ref, out) in enumerate(zip(state_refs, outs))
                ]
            for store in stores:
                store.start()
            for store in stores:
                store.wait()


def attend_call(scale, chunks, who, counts, tokens, parts, queries, buffers, state, tiles=None, last=False):
    layout = tuple(buffer[:3] + (buffer[4],) for buffer in buffers)
    arrays = [buffer[3] for buffer in buffers]
    _, width, rows = queries[0].shape
    n_turn = 2 * (counts.shape[0] // 4)
    heads = counts.shape[0] // 4
    n_units = sum(array.shape[0] - buffer[2] for array, buffer in zip(arrays, buffers))
    state_shapes = [(n_turn, 1, rows), (n_turn, 1, rows), (n_turn, width, rows)]
    if last:
        outs = [jax.ShapeDtypeStruct((tokens // 2, heads * (rows // tokens) * width), jnp.bfloat16)] * 4
    else:
        outs = [jax.ShapeDtypeStruct(shape, jnp.float32) for shape in state_shapes]
    given = [] if state is None else list(state)
    tile_args = [] if tiles is None else list(tiles)
    before = 2 + len(queries) + len(arrays) + len(tile_args)
    aliases = {} if last or state is None else {before + at: at for at in range(3)}
    return pl.pallas_call(
        functools.partial(
            attend_kernel,
            scale,
            chunks,
            layout,
            len(queries),
            tuple(parts),
            len(given),
            last,
        ),
        out_shape=tuple(outs),
        in_specs=[smem(), smem()]
        + [hbm()] * (len(queries) + len(arrays))
        + [vmem()] * len(tile_args)
        + [hbm()] * len(given),
        out_specs=tuple([vmem() if last else hbm()] * len(outs)),
        scratch_shapes=[pltpu.VMEM((n_turn, width, rows), jnp.bfloat16)]
        + [pltpu.VMEM(shape, jnp.float32) for shape in state_shapes]
        + [
            pltpu.VMEM((n_units,) + arrays[0].shape[1:], jnp.bfloat16),
            pltpu.SemaphoreType.DMA((n_units,)),
            pltpu.SemaphoreType.DMA((len(parts), 3)),
            pltpu.SemaphoreType.DMA((len(queries),)),
        ],
        input_output_aliases=aliases,
        compiler_params=pltpu.CompilerParams(vmem_limit_bytes=VMEM),
        cost_estimate=TINY,
    )(who, counts, *queries, *arrays, *tile_args, *given)


def line_of_four(query, new_keys, new_values, memory_keys, memory_values, retrieved):
    queries = query[0]
    tokens, heads, group_size, width = queries.shape
    units_dev = memory_keys.shape[0]
    scale = math.log2(math.e) / math.sqrt(width)
    me = lax.axis_index("mem")
    span = lax.axis_index("span")
    group = lax.axis_index("head")
    low = (me < 2).astype(jnp.int32)
    middle = (me == 1) | (me == 2)
    end = jnp.where(low == 1, 0, 3)
    who = jnp.stack([me, end, 3 - me, 3 - end, low, span > 0, middle, group]).astype(jnp.int32)

    def inward(value):
        return lax.ppermute(value, "mem", [(0, 1), (3, 2)])

    def across(value):
        return lax.ppermute(value, "mem", [(1, 2), (2, 1)])

    def far(value):
        return lax.ppermute(value, "mem", [(0, 2), (3, 1)])

    def onward(value):
        return lax.ppermute(value, "span", [(at, at + 1) for at in range(lax.axis_size("span") - 1)])

    n_mem = lax.axis_size("mem")

    def after(value, before):
        return lax.optimization_barrier((value, before))[0]

    half = heads // 2

    def query_t(value):
        return jnp.transpose(value, (1, 3, 2, 0)).reshape(-1, width, group_size * tokens)

    own_t = [query_t(queries[:, :half])]
    early = inward(own_t[0])
    keys = memory_keys.reshape(units_dev, -1, width)
    values = memory_values.reshape(units_dev, -1, width)
    tile_pair = (new_keys[0].reshape(-1, width), new_values[0].reshape(-1, width))
    unit_lists = after(retrieved[0], own_t[0])
    counts, table, own_0 = gather(who, unit_lists, keys, values, PIECES[:1], 0, tile=tile_pair, n_owner=n_mem)
    stream_0, end_0 = across(own_0), inward(after(own_0, early))
    tile = own_0[:TILE]
    far_tile = far(tile)
    (own_1,) = gather(who, unit_lists, keys, values, PIECES[1:], PIECES[0], table=table)
    end_1 = inward(own_1)
    own_t.append(query_t(after(queries[:, half:], own_1)))
    late = inward(after(own_t[1], end_0))

    places = [sum(PIECES[:at]) for at in range(len(PIECES))]
    starts = [sum(CHUNKS[:at]) for at in range(len(CHUNKS))]
    own = [(OWN, places[0], TILE, own_0), (OWN, places[1], 0, own_1)]
    ends = [(END, places[0], TILE, end_0), (END, places[1], 0, end_1)]
    streams = [(STREAM, starts[0], TILE, stream_0)]
    call = functools.partial(attend_call, scale, CHUNKS, who, counts, tokens)

    def send_chunk(at, sources, state):
        sources = [source[:3] + (after(source[3], state[0]),) for source in sources]
        packed = pack(who, counts, heads, CHUNKS, starts[at], CHUNKS[at], sources)
        streams.append((STREAM, starts[at], 0, across(packed)))
        return [after(state[0], packed), *state[1:]]

    def stage(buffers, before=None):
        if before is not None:
            buffers = [buffer[:3] + (after(buffer[3], before[0]),) for buffer in buffers]
        return [buffer + (0,) for buffer in buffers]

    def parts(tiles, fresh):
        return [(0, heads, 0, tiles, fresh), (heads, 2 * heads, 0, tiles, fresh)]

    mine, first, second = (0, heads), (heads, heads + half), (heads + half, 2 * heads)
    def pinned(buffers, before):
        return [buffer[:3] + (after(buffer[3], before[0]),) for buffer in buffers]

    state = list(call([mine + (0, False, True), first + (0, False, True)], own_t + [early], stage(own), None))
    rest = jnp.concatenate([part[:TILE] for part in (end_0, stream_0, far_tile)])
    tiles = (tile, rest, onward(jnp.concatenate([tile, rest])))
    state = send_chunk(1, own[1:] + ends[:1], state)
    state = list(
        call(
            [mine + (0, False, False), first + (0, False, False)],
            own_t + [early],
            stage(streams[:1] + ends[:1], state),
            state,
        )
    )
    state = send_chunk(2, own[1:] + ends, state)
    late = after(late, state[0])
    both_t = own_t + [early, late]
    state = list(
        call(
            [mine + (1, True, False), first + (1, True, False), second + (0, True, True)],
            both_t,
            stage(own + streams[:1] + ends[:1]) + [buffer + (1,) for buffer in pinned(ends[1:] + streams[1:2], state)],
            state,
            tiles=tiles,
        )
    )
    last_streams = stage(streams[2:], state)
    final = functools.partial(
        call, [mine + (0, False, False), (heads, 2 * heads, 0, False, False)], both_t, last=True
    )

    def fits(piece, state):
        return final(last_streams, state)

    def exceeds(piece, state):
        return final(last_streams + [(EXTRA, places[-1], 0, across(piece), 0)], state)

    by_owner = counts.reshape(-1, heads).sum(axis=1)
    over = jnp.maximum(by_owner[0] + by_owner[1], by_owner[2] + by_owner[3]) > sum(CHUNKS)
    keep_own, send_own, keep_end, send_end = lax.cond(over, exceeds, fits, own_1, tuple(state))

    n_head = lax.axis_size("head")

    def pairs(moves):
        return [
            (source * n_head + at, target * n_head + (at + turn) % n_head)
            for source, target, turn in moves
            for at in range(n_head)
        ]

    axes = ("mem", "head")
    kept = lax.ppermute(keep_end, axes, pairs([(1, 0, 0), (2, 3, 0)]))
    swapped_end = lax.ppermute(send_end, axes, pairs([(1, 0, 1), (2, 3, 1)]))
    swapped_own = lax.ppermute(send_own, axes, pairs([(1, 1, 1), (2, 2, 1)]))
    same = jnp.where(middle, keep_own, kept)
    other = jnp.where(middle, swapped_own, swapped_end)
    left = jnp.where(group == 0, same, other)
    right = jnp.where(group == 0, other, same)
    return jnp.concatenate([left, right], axis=1)[None]


def shifted(value, axis, steps):
    count = lax.axis_size(axis)
    first, last = (max(0, -steps), min(count, count - steps))
    return lax.ppermute(value, axis, [(source, source + steps) for source in range(first, last)])


def any_line(query, new_keys, new_values, memory_keys, memory_values, retrieved):
    queries = query[0]
    row_count, head_count, group_size, head_width = queries.shape
    score_scale = 1.0 / math.sqrt(head_width)
    mem_index = lax.axis_index("mem")
    block_index = lax.axis_index("span")
    row_position = mem_index * row_count + jnp.arange(row_count, dtype=jnp.int32)

    def update(carry_state, key_pair, key_mask):
        old_peak, old_total, old_accum = carry_state
        scores = (
            jnp.einsum("rhgd,khd->rhgk", queries, key_pair[0], preferred_element_type=jnp.float32)
            * score_scale
        )
        scores = jnp.where(key_mask, scores, NEG)
        new_peak = jnp.maximum(old_peak, jnp.max(scores, axis=-1))
        weights = jnp.where(key_mask, jnp.exp(scores - new_peak[..., None]), 0.0)
        factor = jnp.exp(old_peak - new_peak)
        new_total = old_total * factor + jnp.sum(weights, axis=-1)
        new_accum = old_accum * factor[..., None] + jnp.einsum(
            "rhgk,khd->rhgd",
            weights.astype(jnp.bfloat16),
            key_pair[1],
            preferred_element_type=jnp.float32,
        )
        return (new_peak, new_total, new_accum)

    def sweep(carry_state, key_pair, first_key, mask_maker):
        key_count = key_pair.shape[1]
        step_size = key_count if key_count <= 1024 else math.gcd(key_count, 512)

        def advance(step_index, loop_state):
            sub_pair = lax.dynamic_slice_in_dim(key_pair, step_index * step_size, step_size, 1)
            key_position = (
                first_key + step_index * step_size + jnp.arange(step_size, dtype=jnp.int32)
            )
            return update(loop_state, sub_pair, mask_maker(key_position))

        return lax.fori_loop(0, key_count // step_size, advance, carry_state)

    def current_mask(key_position):
        return (key_position[None, :] <= row_position[:, None])[:, None, None, :]

    def prior_mask(key_position):
        return ((key_position[None, :] > row_position[:, None]) & (block_index > 0))[
            :, None, None, :
        ]

    def full_mask(key_position):
        return jnp.ones((1, 1, 1, key_position.shape[0]), bool)

    carry_state = (
        jnp.full((row_count, head_count, group_size), NEG, jnp.float32),
        jnp.zeros((row_count, head_count, group_size), jnp.float32),
        jnp.zeros((row_count, head_count, group_size, head_width), jnp.float32),
    )
    own_pair = jnp.stack([new_keys[0], new_values[0]])
    prior_pair = shifted(own_pair, "span", 1)
    loop_state = carry_state
    first_key = jnp.int32(0)
    loop_state = sweep(
        loop_state, lax.all_gather(own_pair, "mem", axis=1, tiled=True), first_key, current_mask
    )
    carry_state = sweep(
        loop_state, lax.all_gather(prior_pair, "mem", axis=1, tiled=True), first_key, prior_mask
    )
    unit_lists = retrieved[0]
    units_dev = memory_keys.shape[0]
    owners = unit_lists // units_dev
    local_units = unit_lists % units_dev
    owned_here = owners == mem_index
    gathered_pair = []
    for source_array in (memory_keys, memory_values):
        per_head = [
            source_array[local_units[head_at], :, head_at, :] for head_at in range(head_count)
        ]
        gathered_pair.append(jnp.stack(per_head, axis=2))
    gathered_units = jnp.stack(gathered_pair)
    keep_mask = jnp.transpose(owned_here)[None, :, None, :, None]
    slot_terms = jnp.where(keep_mask, gathered_units, jnp.zeros((), jnp.bfloat16))
    slot_terms = slot_terms.reshape(2, -1, head_count, head_width)
    summed_pair = lax.psum(slot_terms, "mem").astype(jnp.float32).astype(jnp.bfloat16)
    carry_state = sweep(carry_state, summed_pair, 0, full_mask)
    final_peak, final_total, final_accum = carry_state
    attended = (final_accum / final_total[..., None]).astype(jnp.bfloat16)
    attended = attended.reshape(row_count, head_count * group_size * head_width)
    moved = lax.all_to_all(attended, "head", split_axis=0, concat_axis=1, tiled=True)
    return moved[None]


def solution(mesh):
    local = line_of_four if mesh.shape["mem"] == 4 and mesh.shape["head"] == 2 else any_line
    return jax.shard_map(
        local,
        mesh=mesh,
        in_specs=(
            P("span", "mem", "head", None, None),
            P("span", "mem", "head", None),
            P("span", "mem", "head", None),
            P("mem", None, "head", None),
            P("mem", None, "head", None),
            P("span", "head", None),
        ),
        out_specs=P("span", ("mem", "head"), None),
        check_vma=False,
    )
```

```python
import functools
import math

import jax
import jax.numpy as jnp
from jax import lax
from jax.experimental import pallas as pl
from jax.experimental.pallas import tpu as pltpu
from jax.sharding import PartitionSpec as P

NEG = -1e30
LANES = 128
VMEM = 56 * 1024 * 1024
TINY = pl.CostEstimate(flops=1000, bytes_accessed=1000, transcendentals=0)
AHEAD = 6

PIECES = (16, 16)
CHUNKS = (16, 16, 16)
FIRST = 16
TILE = 4

ME, ENDER, OPPOSITE, FAR, LOW, PRIOR, MIDDLE, GROUP = range(8)
OWN, END, STREAM, EXTRA = range(4)


def smem():
    return pl.BlockSpec(memory_space=pltpu.SMEM)


def vmem():
    return pl.BlockSpec(memory_space=pltpu.VMEM)


def hbm():
    return pl.BlockSpec(memory_space=pl.ANY)


def head_picker(tokens, rows, head):
    token = lax.broadcasted_iota(jnp.int32, (tokens, rows), 0)
    row = lax.broadcasted_iota(jnp.int32, (tokens, rows), 1)
    return (row == token * (rows // tokens) + head).astype(jnp.bfloat16)


def pick_pair(pick, keys, values):
    keys = jnp.dot(pick, keys, preferred_element_type=jnp.float32)
    values_t = lax.dot_general(
        values, pick, (((0,), (1,)), ((), ())), preferred_element_type=jnp.float32
    )
    return keys.astype(jnp.bfloat16), values_t.astype(jnp.bfloat16)


def plan_units(units_dev, who_ref, list_ref, count_ref, table_ref):
    heads, topk = list_ref.shape
    me = who_ref[ME]

    def clear(at, _):
        count_ref[at] = 0
        return 0

    lax.fori_loop(0, count_ref.shape[0], clear, 0)
    used = jnp.int32(0)
    for head in range(heads):

        def note(at, used, head=head):
            unit = list_ref[head, at]
            owner = lax.div(unit, jnp.int32(units_dev))
            entry = owner * heads + head
            count_ref[entry] = count_ref[entry] + 1
            table_ref[used] = (unit - owner * units_dev) * heads + head
            return used + (owner == me).astype(jnp.int32)

        used = lax.fori_loop(0, topk, note, used)
    table_ref[heads * topk] = used


def gather_kernel(units_dev, pieces, first, tile, who_ref, list_ref, keys_ref, values_ref, *refs):
    refs = list(refs)
    heads, topk = list_ref.shape
    if tile:
        new_keys, new_values, count_ref, table_ref = (refs.pop(0) for _ in range(4))
        plan_units(units_dev, who_ref, list_ref, count_ref, table_ref)
    else:
        table_ref = refs.pop(0)
    outs = [refs.pop(0) for _ in pieces]
    key_buf, value_buf, picks, sems = refs
    rows = keys_ref.shape[1]
    tokens = rows // heads
    used = table_ref[heads * topk]

    def copies(at):
        unit = lax.div(table_ref[at], jnp.int32(heads))
        slot = lax.rem(at, jnp.int32(AHEAD))
        return (
            pltpu.make_async_copy(keys_ref.at[unit], key_buf.at[slot], sems.at[slot, 0]),
            pltpu.make_async_copy(values_ref.at[unit], value_buf.at[slot], sems.at[slot, 1]),
        )

    def start(at, _):
        for copy in copies(at):
            copy.start()
        return 0

    stop = jnp.minimum(used, first + sum(pieces))
    lax.fori_loop(first, jnp.minimum(stop, first + AHEAD), start, 0)
    for head in range(heads):
        picks[head] = head_picker(tokens, rows, head)
    base, place = first, TILE if tile else 0
    if tile:
        for head in range(heads):
            outs[0][head, 0], outs[0][head, 1] = pick_pair(picks[head], new_keys[...], new_values[...])
    for out_ref, size in zip(outs, pieces):

        def item(slot, _, out_ref=out_ref, base=base, place=place):
            at = base + slot
            for copy in copies(at):
                copy.wait()
            here = lax.rem(at, jnp.int32(AHEAD))
            pick = picks[lax.rem(table_ref[at], jnp.int32(heads))]
            out_ref[place + slot, 0], out_ref[place + slot, 1] = pick_pair(
                pick, key_buf[here], value_buf[here]
            )

            @pl.when(at + AHEAD < stop)
            def _():
                start(at + AHEAD, 0)

            return 0

        lax.fori_loop(0, jnp.clip(used - base, 0, size), item, 0)
        base, place = base + size, 0


def gather(who, unit_lists, keys, values, pieces, first, tile=None, table=None, n_owner=None):
    units, rows, width = keys.shape
    heads, topk = unit_lists.shape
    tokens = rows // heads
    extra = [TILE if tile is not None else 0] + [0] * (len(pieces) - 1)
    tables = [
        jax.ShapeDtypeStruct((size,), jnp.int32)
        for size in ([n_owner * heads, heads * topk + 1] if tile is not None else [])
    ]
    return pl.pallas_call(
        functools.partial(gather_kernel, units, pieces, first, tile is not None),
        out_shape=tuple(
            tables
            + [
                jax.ShapeDtypeStruct((size + more, 2, tokens, width), jnp.bfloat16)
                for size, more in zip(pieces, extra)
            ]
        ),
        in_specs=[smem(), smem(), hbm(), hbm()] + ([vmem()] * 2 if tile is not None else [smem()]),
        out_specs=tuple([smem()] * len(tables) + [vmem()] * len(pieces)),
        scratch_shapes=[
            pltpu.VMEM((AHEAD, rows, width), jnp.bfloat16),
            pltpu.VMEM((AHEAD, rows, width), jnp.bfloat16),
            pltpu.VMEM((heads, tokens, rows), jnp.bfloat16),
            pltpu.SemaphoreType.DMA((AHEAD, 2)),
        ],
        compiler_params=pltpu.CompilerParams(vmem_limit_bytes=VMEM),
        cost_estimate=TINY,
    )(who, unit_lists, keys, values, *(tile if tile is not None else (table,)))


def head_ranges(count_ref, heads, owner):
    ranges, at = [], jnp.int32(0)
    for head in range(heads):
        after = at + count_ref[owner * heads + head]
        ranges.append((at, after))
        at = after
    return ranges, at


def stream_shape(chunks, n_middle, n_end):
    extra = jnp.maximum(n_middle + n_end - sum(chunks), 0)
    return extra, jnp.maximum(n_middle - extra, FIRST)


def pack_kernel(heads, chunks, first, layout, who_ref, count_ref, *refs):
    sources = refs[: len(layout)]
    out_ref, sems = refs[len(layout) :]
    size = out_ref.shape[0]

    @pl.when(who_ref[MIDDLE] == 1)
    def _():
        _, n_own = head_ranges(count_ref, heads, who_ref[ME])
        _, n_end = head_ranges(count_ref, heads, who_ref[ENDER])
        extra, base = stream_shape(chunks, n_own, n_end)

        def each(act):
            for (kind, at, skip), ref in zip(layout, sources):
                shift, total = (-extra, n_own) if kind == OWN else (base, n_end)
                count = ref.shape[0] - skip
                low = jnp.maximum(at + shift, first)
                high = jnp.minimum(jnp.minimum(at + count, total) + shift, first + size)

                def one(slot, _, ref=ref, shift=shift, at=at, skip=skip):
                    place = slot - first
                    act(
                        pltpu.make_async_copy(
                            ref.at[slot - shift - at + skip], out_ref.at[place], sems.at[place]
                        )
                    )
                    return 0

                lax.fori_loop(low, jnp.maximum(low, high), one, 0)

        each(lambda copy: copy.start())
        each(lambda copy: copy.wait())


def pack(who, counts, heads, chunks, first, size, sources):
    layout = tuple(source[:3] for source in sources)
    arrays = [source[3] for source in sources]
    return pl.pallas_call(
        functools.partial(pack_kernel, heads, chunks, first, layout),
        out_shape=jax.ShapeDtypeStruct((size,) + arrays[0].shape[1:], jnp.bfloat16),
        in_specs=[smem(), smem()] + [hbm()] * len(arrays),
        out_specs=vmem(),
        scratch_shapes=[pltpu.SemaphoreType.DMA((size,))],
        compiler_params=pltpu.CompilerParams(vmem_limit_bytes=VMEM),
        cost_estimate=TINY,
    )(who, counts, *arrays)


def attend(scale, keys, values_t, queries_t, mask, state):
    peak, total, accum = state
    scores = jnp.dot(keys, queries_t, preferred_element_type=jnp.float32)
    if mask is not None:
        scores = jnp.where(mask, scores, NEG)
    new_peak = jnp.maximum(peak, jnp.max(scores, axis=0, keepdims=True))
    weights = jnp.exp2((scores - new_peak) * scale)
    factor = jnp.exp2((peak - new_peak) * scale)
    total = total * factor + jnp.sum(weights, axis=0, keepdims=True)
    accum = accum * factor + jnp.dot(
        values_t, weights.astype(jnp.bfloat16), preferred_element_type=jnp.float32
    )
    return new_peak, total, accum


def attend_kernel(scale, chunks, layout, n_query, parts, n_state, last, *refs):
    new = any(part[3] for part in parts)
    refs = list(refs)
    who_ref, count_ref = refs.pop(0), refs.pop(0)
    query_in = [refs.pop(0) for _ in range(n_query)]
    buffers = [refs.pop(0) for _ in layout]
    if new:
        cur, prior = refs.pop(0), refs.pop(0)
    state_in = [refs.pop(0) for _ in range(n_state)]
    outs = [refs.pop(0) for _ in range(4 if last else 3)]
    queries, peak_ref, total_ref, accum_ref, units, unit_sems, state_sems, query_sems = refs
    state_refs = (peak_ref, total_ref, accum_ref)
    n_turn, width, rows = queries.shape
    tokens = units.shape[2]
    heads = list(count_ref.shape)[0] // 4

    def update(turn, keys, values_t, mask=None):
        for start in range(0, rows, LANES):
            lanes = pl.ds(start, LANES)
            state = tuple(ref[turn, :, lanes] for ref in state_refs)
            state = attend(scale, keys, values_t, queries[turn, :, lanes], mask, state)
            for ref, part in zip(state_refs, state):
                ref[turn, :, lanes] = part

    def new_tiles(turn, head, group):
        low, has_prior = who_ref[LOW] == 1, who_ref[PRIOR] == 1

        def tile(ref, at=0):
            return ref[at * TILE + head, 0], ref[at * TILE + head, 1]

        def choose(flag, yes, no):
            return tuple(jnp.where(flag, a, b) for a, b in zip(yes, no))

        def join(a, b):
            return jnp.concatenate([a[0], b[0]], axis=0), jnp.concatenate([a[1], b[1]], axis=1)

        key = lax.broadcasted_iota(jnp.int32, (2 * tokens, LANES), 0)
        position = lax.broadcasted_iota(jnp.int32, (2 * tokens, LANES), 1) % tokens
        mask = ((key < tokens) & (key <= position)) | (
            (key >= tokens) & (key - tokens > position) & has_prior
        )

        def both():
            pairs = [choose(low, tile(prior, at), tile(cur, at)) for at in (2, 3)]
            update(turn, *join(*pairs))

        if group == 0:
            update(turn, *join(tile(cur), tile(prior)), mask)

            @pl.when(low | has_prior)
            def _():
                update(turn, *choose(low, tile(cur, 1), tile(prior, 1)))

            pl.when(jnp.logical_not(low) | has_prior)(both)
        else:
            update(turn, *join(tile(cur, 1), tile(prior, 1)), mask)

            @pl.when(jnp.logical_not(low) | has_prior)
            def _():
                update(turn, *choose(low, tile(prior), tile(cur)))
                both()

    @pl.when(who_ref[MIDDLE] == 1)
    def _():
        loads = []
        at = parts[0][0]
        for number, ref in enumerate(query_in):
            here = pl.ds(at, ref.shape[0])
            loads.append(pltpu.make_async_copy(ref, queries.at[here], query_sems.at[number]))
            at += ref.shape[0]
        for number, (lowest, highest, _, _, fresh) in enumerate(parts):
            if not fresh:
                here = pl.ds(lowest, highest - lowest)
                loads += [
                    pltpu.make_async_copy(source.at[here], ref.at[here], state_sems.at[number, at])
                    for at, (source, ref) in enumerate(zip(state_in, state_refs))
                ]
        for load in loads:
            load.start()

        ranges, totals = zip(
            *(head_ranges(count_ref, heads, who_ref[role]) for role in (ME, ENDER, OPPOSITE, FAR))
        )
        extra, base = stream_shape(chunks, totals[2], totals[3])
        n_stage = max(entry[3] for entry in layout) + 1
        place, bounds = jnp.int32(0), []
        for head in range(heads):
            stage_at = -1
            for (kind, first, skip, stage), buffer in zip(layout, buffers):
                while stage_at < stage:
                    stage_at += 1
                    bounds.append(place)
                if kind == STREAM:
                    low, high = ranges[2][head]
                    spans = [
                        (low, jnp.minimum(high, FIRST)),
                        (jnp.maximum(low, FIRST + extra) - extra, high - extra),
                    ]
                    low, high = ranges[3][head]
                    spans.append((base + low, base + high))
                elif kind == EXTRA:
                    low, high = ranges[2][head]
                    spans = [(jnp.maximum(low, FIRST), jnp.minimum(high, FIRST + extra))]
                else:
                    spans = [ranges[0 if kind == OWN else 1][head]]
                for low, high in spans:
                    low = jnp.maximum(low - first, 0)
                    high = jnp.maximum(jnp.minimum(high - first, buffer.shape[0] - skip), low)

                    def fetch(at, _, buffer=buffer, skip=skip, shift=place - low):
                        slot = at + shift
                        pltpu.make_async_copy(
                            buffer.at[at + skip], units.at[slot], unit_sems.at[slot]
                        ).start()
                        return 0

                    lax.fori_loop(low, high, fetch, 0)
                    place = place + high - low
            bounds.append(place)

        def arrived(slot, _):
            pltpu.make_async_copy(buffers[0].at[0], units.at[slot], unit_sems.at[slot]).wait()
            return 0

        lax.fori_loop(0, place, arrived, 0)
        for load in loads:
            load.wait()

        def one_turn(turn, _, group, stage, tiles, fresh):
            head = lax.rem(turn, jnp.int32(heads))
            if fresh:
                peak_ref[turn] = jnp.full((1, rows), NEG, jnp.float32)
                total_ref[turn] = jnp.zeros((1, rows), jnp.float32)
                accum_ref[turn] = jnp.zeros((width, rows), jnp.float32)
            if tiles:
                new_tiles(turn, head, group)
            low, high = jnp.int32(0), jnp.int32(0)
            for at in range(heads):
                low = jnp.where(head == at, bounds[at * (n_stage + 1) + stage], low)
                high = jnp.where(head == at, bounds[at * (n_stage + 1) + n_stage], high)

            def several(slot, count):
                keys = units[pl.ds(slot, count), 0].reshape(count * tokens, width)
                values_t = jnp.concatenate([units[slot + at, 1] for at in range(count)], axis=1)
                update(turn, keys, values_t)

            fours = lax.div(high - low, jnp.int32(4))

            def four(at, _):
                several(low + 4 * at, 4)
                return 0

            lax.fori_loop(0, fours, four, 0)
            left = high - low - 4 * fours

            @pl.when(left >= 2)
            def _():
                several(high - left, 2)

            @pl.when((left == 1) | (left == 3))
            def _():
                several(high - 1, 1)

            if last:
                keep_own, send_own, keep_end, send_end = outs
                half = tokens // 2
                first_group = who_ref[GROUP] == 0
                for own_rows, keep_ref, send_ref in (
                    (True, keep_own, send_own),
                    (False, keep_end, send_end),
                ):

                    @pl.when((turn < heads) == own_rows)
                    def _(keep_ref=keep_ref, send_ref=send_ref):
                        for member in range(rows // tokens):
                            lanes = pl.ds(member * tokens, tokens)
                            result = accum_ref[turn, :, lanes] / total_ref[turn, :, lanes]
                            result = result.T
                            top, bottom = result[:half], result[half:]
                            column = pl.ds(
                                pl.multiple_of((head * (rows // tokens) + member) * width, width), width
                            )
                            keep_ref[:, column] = jnp.where(first_group, top, bottom).astype(jnp.bfloat16)
                            send_ref[:, column] = jnp.where(first_group, bottom, top).astype(jnp.bfloat16)

            return 0

        for lowest, highest, stage, tiles, fresh in parts:
            body = functools.partial(
                one_turn, group=0 if lowest < heads else 1, stage=stage, tiles=tiles, fresh=fresh
            )
            lax.fori_loop(lowest, highest, body, 0)
        if not last:
            stores = []
            for number, (lowest, highest, _, _, _) in enumerate(parts):
                here = pl.ds(lowest, highest - lowest)
                stores += [
                    pltpu.make_async_copy(ref.at[here], out.at[here], state_sems.at[number, at])
                    for at, (ref, out) in enumerate(zip(state_refs, outs))
                ]
            for store in stores:
                store.start()
            for store in stores:
                store.wait()


def attend_call(scale, chunks, who, counts, tokens, parts, queries, buffers, state, tiles=None, last=False):
    layout = tuple(buffer[:3] + (buffer[4],) for buffer in buffers)
    arrays = [buffer[3] for buffer in buffers]
    _, width, rows = queries[0].shape
    n_turn = 2 * (counts.shape[0] // 4)
    heads = counts.shape[0] // 4
    n_units = sum(array.shape[0] - buffer[2] for array, buffer in zip(arrays, buffers))
    state_shapes = [(n_turn, 1, rows), (n_turn, 1, rows), (n_turn, width, rows)]
    if last:
        outs = [jax.ShapeDtypeStruct((tokens // 2, heads * (rows // tokens) * width), jnp.bfloat16)] * 4
    else:
        outs = [jax.ShapeDtypeStruct(shape, jnp.float32) for shape in state_shapes]
    given = [] if state is None else list(state)
    tile_args = [] if tiles is None else list(tiles)
    before = 2 + len(queries) + len(arrays) + len(tile_args)
    aliases = {} if last or state is None else {before + at: at for at in range(3)}
    return pl.pallas_call(
        functools.partial(
            attend_kernel,
            scale,
            chunks,
            layout,
            len(queries),
            tuple(parts),
            len(given),
            last,
        ),
        out_shape=tuple(outs),
        in_specs=[smem(), smem()]
        + [hbm()] * (len(queries) + len(arrays))
        + [vmem()] * len(tile_args)
        + [hbm()] * len(given),
        out_specs=tuple([vmem() if last else hbm()] * len(outs)),
        scratch_shapes=[pltpu.VMEM((n_turn, width, rows), jnp.bfloat16)]
        + [pltpu.VMEM(shape, jnp.float32) for shape in state_shapes]
        + [
            pltpu.VMEM((n_units,) + arrays[0].shape[1:], jnp.bfloat16),
            pltpu.SemaphoreType.DMA((n_units,)),
            pltpu.SemaphoreType.DMA((len(parts), 3)),
            pltpu.SemaphoreType.DMA((len(queries),)),
        ],
        input_output_aliases=aliases,
        compiler_params=pltpu.CompilerParams(vmem_limit_bytes=VMEM),
        cost_estimate=TINY,
    )(who, counts, *queries, *arrays, *tile_args, *given)


def line_of_four(query, new_keys, new_values, memory_keys, memory_values, retrieved):
    queries = query[0]
    tokens, heads, group_size, width = queries.shape
    units_dev = memory_keys.shape[0]
    scale = math.log2(math.e) / math.sqrt(width)
    me = lax.axis_index("mem")
    span = lax.axis_index("span")
    group = lax.axis_index("head")
    low = (me < 2).astype(jnp.int32)
    middle = (me == 1) | (me == 2)
    end = jnp.where(low == 1, 0, 3)
    who = jnp.stack([me, end, 3 - me, 3 - end, low, span > 0, middle, group]).astype(jnp.int32)

    def inward(value):
        return lax.ppermute(value, "mem", [(0, 1), (3, 2)])

    def across(value):
        return lax.ppermute(value, "mem", [(1, 2), (2, 1)])

    def far(value):
        return lax.ppermute(value, "mem", [(0, 2), (3, 1)])

    def onward(value):
        return lax.ppermute(value, "span", [(at, at + 1) for at in range(lax.axis_size("span") - 1)])

    n_mem = lax.axis_size("mem")

    def after(value, before):
        return lax.optimization_barrier((value, before))[0]

    half = heads // 2

    def query_t(value):
        return jnp.transpose(value, (1, 3, 2, 0)).reshape(-1, width, group_size * tokens)

    own_t = [query_t(queries[:, :half])]
    early = inward(own_t[0])
    keys = memory_keys.reshape(units_dev, -1, width)
    values = memory_values.reshape(units_dev, -1, width)
    tile_pair = (new_keys[0].reshape(-1, width), new_values[0].reshape(-1, width))
    unit_lists = after(retrieved[0], own_t[0])
    counts, table, own_0 = gather(who, unit_lists, keys, values, PIECES[:1], 0, tile=tile_pair, n_owner=n_mem)
    stream_0, end_0 = across(own_0), inward(after(own_0, early))
    tile = own_0[:TILE]
    far_tile = far(tile)
    (own_1,) = gather(who, unit_lists, keys, values, PIECES[1:], PIECES[0], table=table)
    end_1 = inward(own_1)
    own_t.append(query_t(after(queries[:, half:], own_1)))
    late = inward(after(own_t[1], end_0))

    places = [sum(PIECES[:at]) for at in range(len(PIECES))]
    starts = [sum(CHUNKS[:at]) for at in range(len(CHUNKS))]
    own = [(OWN, places[0], TILE, own_0), (OWN, places[1], 0, own_1)]
    ends = [(END, places[0], TILE, end_0), (END, places[1], 0, end_1)]
    streams = [(STREAM, starts[0], TILE, stream_0)]
    call = functools.partial(attend_call, scale, CHUNKS, who, counts, tokens)

    def send_chunk(at, sources, state):
        sources = [source[:3] + (after(source[3], state[0]),) for source in sources]
        packed = pack(who, counts, heads, CHUNKS, starts[at], CHUNKS[at], sources)
        streams.append((STREAM, starts[at], 0, across(packed)))
        return [after(state[0], packed), *state[1:]]

    def stage(buffers, before=None):
        if before is not None:
            buffers = [buffer[:3] + (after(buffer[3], before[0]),) for buffer in buffers]
        return [buffer + (0,) for buffer in buffers]

    def parts(tiles, fresh):
        return [(0, heads, 0, tiles, fresh), (heads, 2 * heads, 0, tiles, fresh)]

    mine, first, second = (0, heads), (heads, heads + half), (heads + half, 2 * heads)
    def pinned(buffers, before):
        return [buffer[:3] + (after(buffer[3], before[0]),) for buffer in buffers]

    by_owner = counts.reshape(-1, heads).sum(axis=1)
    over = jnp.maximum(by_owner[0] + by_owner[1], by_owner[2] + by_owner[3]) > sum(CHUNKS)
    own_t[0] = after(own_t[0], over)
    state = list(call([mine + (0, False, True), first + (0, False, True)], own_t + [early], stage(own), None))
    state = send_chunk(1, own[1:] + ends[:1], state)
    state = list(
        call(
            [mine + (0, False, False), first + (0, False, False)],
            own_t + [early],
            stage(streams[:1] + ends[:1], state),
            state,
        )
    )
    tiles = jnp.concatenate([own_0[:TILE], end_0[:TILE], stream_0[:TILE], after(far_tile, state[0])])
    tiles = (tiles, onward(tiles))
    state = send_chunk(2, own[1:] + ends, state)
    state = list(
        call(
            [mine + (0, True, False), first + (0, True, False)],
            own_t + [early],
            stage(ends[1:] + streams[1:2], state),
            state, tiles=tiles,
        )
    )
    late = after(late, state[0])
    both_t = own_t + [early, late]
    state = list(
        call(
            [second + (0, True, True)],
            [late],
            stage(own + streams[:1] + ends + streams[1:2], state),
            state,
            tiles=tiles,
        )
    )
    last_streams = stage(streams[2:], state)
    final = functools.partial(
        call, [mine + (0, False, False), (heads, 2 * heads, 0, False, False)], both_t, last=True
    )

    def fits(piece, state):
        return final(last_streams, state)

    def exceeds(piece, state):
        return final(last_streams + [(EXTRA, places[-1], 0, across(piece), 0)], state)

    keep_own, send_own, keep_end, send_end = lax.cond(over, exceeds, fits, own_1, tuple(state))

    n_head = lax.axis_size("head")

    def pairs(moves):
        return [
            (source * n_head + at, target * n_head + (at + turn) % n_head)
            for source, target, turn in moves
            for at in range(n_head)
        ]

    axes = ("mem", "head")
    kept = lax.ppermute(keep_end, axes, pairs([(1, 0, 0), (2, 3, 0)]))
    swapped_end = lax.ppermute(send_end, axes, pairs([(1, 0, 1), (2, 3, 1)]))
    swapped_own = lax.ppermute(send_own, axes, pairs([(1, 1, 1), (2, 2, 1)]))
    same = jnp.where(middle, keep_own, kept)
    other = jnp.where(middle, swapped_own, swapped_end)
    left = jnp.where(group == 0, same, other)
    right = jnp.where(group == 0, other, same)
    return jnp.concatenate([left, right], axis=1)[None]


def shifted(value, axis, steps):
    count = lax.axis_size(axis)
    first, last = (max(0, -steps), min(count, count - steps))
    return lax.ppermute(value, axis, [(source, source + steps) for source in range(first, last)])


def any_line(query, new_keys, new_values, memory_keys, memory_values, retrieved):
    queries = query[0]
    row_count, head_count, group_size, head_width = queries.shape
    score_scale = 1.0 / math.sqrt(head_width)
    mem_index = lax.axis_index("mem")
    block_index = lax.axis_index("span")
    row_position = mem_index * row_count + jnp.arange(row_count, dtype=jnp.int32)

    def update(carry_state, key_pair, key_mask):
        old_peak, old_total, old_accum = carry_state
        scores = (
            jnp.einsum("rhgd,khd->rhgk", queries, key_pair[0], preferred_element_type=jnp.float32)
            * score_scale
        )
        scores = jnp.where(key_mask, scores, NEG)
        new_peak = jnp.maximum(old_peak, jnp.max(scores, axis=-1))
        weights = jnp.where(key_mask, jnp.exp(scores - new_peak[..., None]), 0.0)
        factor = jnp.exp(old_peak - new_peak)
        new_total = old_total * factor + jnp.sum(weights, axis=-1)
        new_accum = old_accum * factor[..., None] + jnp.einsum(
            "rhgk,khd->rhgd",
            weights.astype(jnp.bfloat16),
            key_pair[1],
            preferred_element_type=jnp.float32,
        )
        return (new_peak, new_total, new_accum)

    def sweep(carry_state, key_pair, first_key, mask_maker):
        key_count = key_pair.shape[1]
        step_size = key_count if key_count <= 1024 else math.gcd(key_count, 512)

        def advance(step_index, loop_state):
            sub_pair = lax.dynamic_slice_in_dim(key_pair, step_index * step_size, step_size, 1)
            key_position = (
                first_key + step_index * step_size + jnp.arange(step_size, dtype=jnp.int32)
            )
            return update(loop_state, sub_pair, mask_maker(key_position))

        return lax.fori_loop(0, key_count // step_size, advance, carry_state)

    def current_mask(key_position):
        return (key_position[None, :] <= row_position[:, None])[:, None, None, :]

    def prior_mask(key_position):
        return ((key_position[None, :] > row_position[:, None]) & (block_index > 0))[
            :, None, None, :
        ]

    def full_mask(key_position):
        return jnp.ones((1, 1, 1, key_position.shape[0]), bool)

    carry_state = (
        jnp.full((row_count, head_count, group_size), NEG, jnp.float32),
        jnp.zeros((row_count, head_count, group_size), jnp.float32),
        jnp.zeros((row_count, head_count, group_size, head_width), jnp.float32),
    )
    own_pair = jnp.stack([new_keys[0], new_values[0]])
    prior_pair = shifted(own_pair, "span", 1)
    loop_state = carry_state
    first_key = jnp.int32(0)
    loop_state = sweep(
        loop_state, lax.all_gather(own_pair, "mem", axis=1, tiled=True), first_key, current_mask
    )
    carry_state = sweep(
        loop_state, lax.all_gather(prior_pair, "mem", axis=1, tiled=True), first_key, prior_mask
    )
    unit_lists = retrieved[0]
    units_dev = memory_keys.shape[0]
    owners = unit_lists // units_dev
    local_units = unit_lists % units_dev
    owned_here = owners == mem_index
    gathered_pair = []
    for source_array in (memory_keys, memory_values):
        per_head = [
            source_array[local_units[head_at], :, head_at, :] for head_at in range(head_count)
        ]
        gathered_pair.append(jnp.stack(per_head, axis=2))
    gathered_units = jnp.stack(gathered_pair)
    keep_mask = jnp.transpose(owned_here)[None, :, None, :, None]
    slot_terms = jnp.where(keep_mask, gathered_units, jnp.zeros((), jnp.bfloat16))
    slot_terms = slot_terms.reshape(2, -1, head_count, head_width)
    summed_pair = lax.psum(slot_terms, "mem").astype(jnp.float32).astype(jnp.bfloat16)
    carry_state = sweep(carry_state, summed_pair, 0, full_mask)
    final_peak, final_total, final_accum = carry_state
    attended = (final_accum / final_total[..., None]).astype(jnp.bfloat16)
    attended = attended.reshape(row_count, head_count * group_size * head_width)
    moved = lax.all_to_all(attended, "head", split_axis=0, concat_axis=1, tiled=True)
    return moved[None]


def solution(mesh):
    local = line_of_four if mesh.shape["mem"] == 4 and mesh.shape["head"] == 2 else any_line
    return jax.shard_map(
        local,
        mesh=mesh,
        in_specs=(
            P("span", "mem", "head", None, None),
            P("span", "mem", "head", None),
            P("span", "mem", "head", None),
            P("mem", None, "head", None),
            P("mem", None, "head", None),
            P("span", "head", None),
        ),
        out_specs=P("span", ("mem", "head"), None),
        check_vma=False,
    )
```

```python
import functools
import math

import jax
import jax.numpy as jnp
from jax import lax
from jax.experimental import pallas as pl
from jax.experimental.pallas import tpu as pltpu
from jax.sharding import PartitionSpec as P

NEG = -1e30
LANES = 128
VMEM = 56 * 1024 * 1024
TINY = pl.CostEstimate(flops=1000, bytes_accessed=1000, transcendentals=0)
AHEAD = 6

PIECES = (16, 16)
CHUNKS = (16, 16, 16)
FIRST = 16
TILE = 4

ME, ENDER, OPPOSITE, FAR, LOW, PRIOR, MIDDLE, GROUP = range(8)
OWN, END, STREAM, EXTRA = range(4)


def smem():
    return pl.BlockSpec(memory_space=pltpu.SMEM)


def vmem():
    return pl.BlockSpec(memory_space=pltpu.VMEM)


def hbm():
    return pl.BlockSpec(memory_space=pl.ANY)


def head_picker(tokens, rows, head):
    token = lax.broadcasted_iota(jnp.int32, (tokens, rows), 0)
    row = lax.broadcasted_iota(jnp.int32, (tokens, rows), 1)
    return (row == token * (rows // tokens) + head).astype(jnp.bfloat16)


def pick_pair(pick, keys, values):
    keys = jnp.dot(pick, keys, preferred_element_type=jnp.float32)
    values_t = lax.dot_general(
        values, pick, (((0,), (1,)), ((), ())), preferred_element_type=jnp.float32
    )
    return keys.astype(jnp.bfloat16), values_t.astype(jnp.bfloat16)


def plan_units(units_dev, who_ref, list_ref, count_ref, table_ref):
    heads, topk = list_ref.shape
    me = who_ref[ME]

    def clear(at, _):
        count_ref[at] = 0
        return 0

    lax.fori_loop(0, count_ref.shape[0], clear, 0)
    used = jnp.int32(0)
    for head in range(heads):

        def note(at, used, head=head):
            unit = list_ref[head, at]
            owner = lax.div(unit, jnp.int32(units_dev))
            entry = owner * heads + head
            count_ref[entry] = count_ref[entry] + 1
            table_ref[used] = (unit - owner * units_dev) * heads + head
            return used + (owner == me).astype(jnp.int32)

        used = lax.fori_loop(0, topk, note, used)
    table_ref[heads * topk] = used


def gather_kernel(units_dev, pieces, first, tile, who_ref, list_ref, keys_ref, values_ref, *refs):
    refs = list(refs)
    heads, topk = list_ref.shape
    if tile:
        new_keys, new_values, count_ref, table_ref = (refs.pop(0) for _ in range(4))
        plan_units(units_dev, who_ref, list_ref, count_ref, table_ref)
    else:
        table_ref = refs.pop(0)
    outs = [refs.pop(0) for _ in pieces]
    key_buf, value_buf, picks, sems = refs
    rows = keys_ref.shape[1]
    tokens = rows // heads
    used = table_ref[heads * topk]

    def copies(at):
        unit = lax.div(table_ref[at], jnp.int32(heads))
        slot = lax.rem(at, jnp.int32(AHEAD))
        return (
            pltpu.make_async_copy(keys_ref.at[unit], key_buf.at[slot], sems.at[slot, 0]),
            pltpu.make_async_copy(values_ref.at[unit], value_buf.at[slot], sems.at[slot, 1]),
        )

    def start(at, _):
        for copy in copies(at):
            copy.start()
        return 0

    stop = jnp.minimum(used, first + sum(pieces))
    lax.fori_loop(first, jnp.minimum(stop, first + AHEAD), start, 0)
    for head in range(heads):
        picks[head] = head_picker(tokens, rows, head)
    base, place = first, TILE if tile else 0
    if tile:
        for head in range(heads):
            outs[0][head, 0], outs[0][head, 1] = pick_pair(picks[head], new_keys[...], new_values[...])
    for out_ref, size in zip(outs, pieces):

        def item(slot, _, out_ref=out_ref, base=base, place=place):
            at = base + slot
            for copy in copies(at):
                copy.wait()
            here = lax.rem(at, jnp.int32(AHEAD))
            pick = picks[lax.rem(table_ref[at], jnp.int32(heads))]
            out_ref[place + slot, 0], out_ref[place + slot, 1] = pick_pair(
                pick, key_buf[here], value_buf[here]
            )

            @pl.when(at + AHEAD < stop)
            def _():
                start(at + AHEAD, 0)

            return 0

        lax.fori_loop(0, jnp.clip(used - base, 0, size), item, 0)
        base, place = base + size, 0


def gather(who, unit_lists, keys, values, pieces, first, tile=None, table=None, n_owner=None):
    units, rows, width = keys.shape
    heads, topk = unit_lists.shape
    tokens = rows // heads
    extra = [TILE if tile is not None else 0] + [0] * (len(pieces) - 1)
    tables = [
        jax.ShapeDtypeStruct((size,), jnp.int32)
        for size in ([n_owner * heads, heads * topk + 1] if tile is not None else [])
    ]
    return pl.pallas_call(
        functools.partial(gather_kernel, units, pieces, first, tile is not None),
        out_shape=tuple(
            tables
            + [
                jax.ShapeDtypeStruct((size + more, 2, tokens, width), jnp.bfloat16)
                for size, more in zip(pieces, extra)
            ]
        ),
        in_specs=[smem(), smem(), hbm(), hbm()] + ([vmem()] * 2 if tile is not None else [smem()]),
        out_specs=tuple([smem()] * len(tables) + [vmem()] * len(pieces)),
        scratch_shapes=[
            pltpu.VMEM((AHEAD, rows, width), jnp.bfloat16),
            pltpu.VMEM((AHEAD, rows, width), jnp.bfloat16),
            pltpu.VMEM((heads, tokens, rows), jnp.bfloat16),
            pltpu.SemaphoreType.DMA((AHEAD, 2)),
        ],
        compiler_params=pltpu.CompilerParams(vmem_limit_bytes=VMEM),
        cost_estimate=TINY,
    )(who, unit_lists, keys, values, *(tile if tile is not None else (table,)))


def head_ranges(count_ref, heads, owner):
    ranges, at = [], jnp.int32(0)
    for head in range(heads):
        after = at + count_ref[owner * heads + head]
        ranges.append((at, after))
        at = after
    return ranges, at


def stream_shape(chunks, n_middle, n_end):
    extra = jnp.maximum(n_middle + n_end - sum(chunks), 0)
    return extra, jnp.maximum(n_middle - extra, FIRST)


def pack_kernel(heads, chunks, first, layout, who_ref, count_ref, *refs):
    sources = refs[: len(layout)]
    out_ref, sems = refs[len(layout) :]
    size = out_ref.shape[0]

    @pl.when(who_ref[MIDDLE] == 1)
    def _():
        _, n_own = head_ranges(count_ref, heads, who_ref[ME])
        _, n_end = head_ranges(count_ref, heads, who_ref[ENDER])
        extra, base = stream_shape(chunks, n_own, n_end)

        def each(act):
            for (kind, at, skip), ref in zip(layout, sources):
                shift, total = (-extra, n_own) if kind == OWN else (base, n_end)
                count = ref.shape[0] - skip
                low = jnp.maximum(at + shift, first)
                high = jnp.minimum(jnp.minimum(at + count, total) + shift, first + size)

                def one(slot, _, ref=ref, shift=shift, at=at, skip=skip):
                    place = slot - first
                    act(
                        pltpu.make_async_copy(
                            ref.at[slot - shift - at + skip], out_ref.at[place], sems.at[place]
                        )
                    )
                    return 0

                lax.fori_loop(low, jnp.maximum(low, high), one, 0)

        each(lambda copy: copy.start())
        each(lambda copy: copy.wait())


def pack(who, counts, heads, chunks, first, size, sources):
    layout = tuple(source[:3] for source in sources)
    arrays = [source[3] for source in sources]
    return pl.pallas_call(
        functools.partial(pack_kernel, heads, chunks, first, layout),
        out_shape=jax.ShapeDtypeStruct((size,) + arrays[0].shape[1:], jnp.bfloat16),
        in_specs=[smem(), smem()] + [hbm()] * len(arrays),
        out_specs=vmem(),
        scratch_shapes=[pltpu.SemaphoreType.DMA((size,))],
        compiler_params=pltpu.CompilerParams(vmem_limit_bytes=VMEM),
        cost_estimate=TINY,
    )(who, counts, *arrays)


def attend(scale, keys, values_t, queries_t, mask, state):
    peak, total, accum = state
    scores = jnp.dot(keys, queries_t, preferred_element_type=jnp.float32)
    if mask is not None:
        scores = jnp.where(mask, scores, NEG)
    new_peak = jnp.maximum(peak, jnp.max(scores, axis=0, keepdims=True))
    weights = jnp.exp2((scores - new_peak) * scale)
    factor = jnp.exp2((peak - new_peak) * scale)
    total = total * factor + jnp.sum(weights, axis=0, keepdims=True)
    accum = accum * factor + jnp.dot(
        values_t, weights.astype(jnp.bfloat16), preferred_element_type=jnp.float32
    )
    return new_peak, total, accum


def attend_kernel(scale, chunks, layout, n_query, parts, n_state, last, *refs):
    new = any(part[3] for part in parts)
    refs = list(refs)
    who_ref, count_ref = refs.pop(0), refs.pop(0)
    query_in = [refs.pop(0) for _ in range(n_query)]
    buffers = [refs.pop(0) for _ in layout]
    if new:
        cur, prior = refs.pop(0), refs.pop(0)
    state_in = [refs.pop(0) for _ in range(n_state)]
    outs = [refs.pop(0) for _ in range(4 if last else 3)]
    queries, peak_ref, total_ref, accum_ref, units, unit_sems, state_sems, query_sems = refs
    state_refs = (peak_ref, total_ref, accum_ref)
    n_turn, width, rows = queries.shape
    tokens = units.shape[2]
    heads = list(count_ref.shape)[0] // 4

    def update(turn, keys, values_t, mask=None):
        for start in range(0, rows, LANES):
            lanes = pl.ds(start, LANES)
            state = tuple(ref[turn, :, lanes] for ref in state_refs)
            state = attend(scale, keys, values_t, queries[turn, :, lanes], mask, state)
            for ref, part in zip(state_refs, state):
                ref[turn, :, lanes] = part

    def new_tiles(turn, head, group):
        low, has_prior = who_ref[LOW] == 1, who_ref[PRIOR] == 1

        def tile(ref, at=0):
            return ref[at * TILE + head, 0], ref[at * TILE + head, 1]

        def choose(flag, yes, no):
            return tuple(jnp.where(flag, a, b) for a, b in zip(yes, no))

        def join(a, b):
            return jnp.concatenate([a[0], b[0]], axis=0), jnp.concatenate([a[1], b[1]], axis=1)

        key = lax.broadcasted_iota(jnp.int32, (2 * tokens, LANES), 0)
        position = lax.broadcasted_iota(jnp.int32, (2 * tokens, LANES), 1) % tokens
        mask = ((key < tokens) & (key <= position)) | (
            (key >= tokens) & (key - tokens > position) & has_prior
        )

        def both():
            pairs = [choose(low, tile(prior, at), tile(cur, at)) for at in (2, 3)]
            update(turn, *join(*pairs))

        if group == 0:
            update(turn, *join(tile(cur), tile(prior)), mask)

            @pl.when(low | has_prior)
            def _():
                update(turn, *choose(low, tile(cur, 1), tile(prior, 1)))

            pl.when(jnp.logical_not(low) | has_prior)(both)
        else:
            update(turn, *join(tile(cur, 1), tile(prior, 1)), mask)

            @pl.when(jnp.logical_not(low) | has_prior)
            def _():
                update(turn, *choose(low, tile(prior), tile(cur)))
                both()

    @pl.when(who_ref[MIDDLE] == 1)
    def _():
        loads = []
        at = parts[0][0]
        for number, ref in enumerate(query_in):
            here = pl.ds(at, ref.shape[0])
            loads.append(pltpu.make_async_copy(ref, queries.at[here], query_sems.at[number]))
            at += ref.shape[0]
        for number, (lowest, highest, _, _, fresh) in enumerate(parts):
            if not fresh:
                here = pl.ds(lowest, highest - lowest)
                loads += [
                    pltpu.make_async_copy(source.at[here], ref.at[here], state_sems.at[number, at])
                    for at, (source, ref) in enumerate(zip(state_in, state_refs))
                ]
        for load in loads:
            load.start()

        ranges, totals = zip(
            *(head_ranges(count_ref, heads, who_ref[role]) for role in (ME, ENDER, OPPOSITE, FAR))
        )
        extra, base = stream_shape(chunks, totals[2], totals[3])
        n_stage = max(entry[3] for entry in layout) + 1
        place, bounds = jnp.int32(0), []
        for head in range(heads):
            stage_at = -1
            for (kind, first, skip, stage), buffer in zip(layout, buffers):
                while stage_at < stage:
                    stage_at += 1
                    bounds.append(place)
                if kind == STREAM:
                    low, high = ranges[2][head]
                    spans = [
                        (low, jnp.minimum(high, FIRST)),
                        (jnp.maximum(low, FIRST + extra) - extra, high - extra),
                    ]
                    low, high = ranges[3][head]
                    spans.append((base + low, base + high))
                elif kind == EXTRA:
                    low, high = ranges[2][head]
                    spans = [(jnp.maximum(low, FIRST), jnp.minimum(high, FIRST + extra))]
                else:
                    spans = [ranges[0 if kind == OWN else 1][head]]
                for low, high in spans:
                    low = jnp.maximum(low - first, 0)
                    high = jnp.maximum(jnp.minimum(high - first, buffer.shape[0] - skip), low)

                    def fetch(at, _, buffer=buffer, skip=skip, shift=place - low):
                        slot = at + shift
                        pltpu.make_async_copy(
                            buffer.at[at + skip], units.at[slot], unit_sems.at[slot]
                        ).start()
                        return 0

                    lax.fori_loop(low, high, fetch, 0)
                    place = place + high - low
            bounds.append(place)

        def arrived(slot, _):
            pltpu.make_async_copy(buffers[0].at[0], units.at[slot], unit_sems.at[slot]).wait()
            return 0

        lax.fori_loop(0, place, arrived, 0)
        for load in loads:
            load.wait()

        def one_turn(turn, _, group, stage, tiles, fresh):
            head = lax.rem(turn, jnp.int32(heads))
            if fresh:
                peak_ref[turn] = jnp.full((1, rows), NEG, jnp.float32)
                total_ref[turn] = jnp.zeros((1, rows), jnp.float32)
                accum_ref[turn] = jnp.zeros((width, rows), jnp.float32)
            if tiles:
                new_tiles(turn, head, group)
            low, high = jnp.int32(0), jnp.int32(0)
            for at in range(heads):
                low = jnp.where(head == at, bounds[at * (n_stage + 1) + stage], low)
                high = jnp.where(head == at, bounds[at * (n_stage + 1) + n_stage], high)

            def several(slot, count):
                keys = units[pl.ds(slot, count), 0].reshape(count * tokens, width)
                values_t = jnp.concatenate([units[slot + at, 1] for at in range(count)], axis=1)
                update(turn, keys, values_t)

            fours = lax.div(high - low, jnp.int32(4))

            def four(at, _):
                several(low + 4 * at, 4)
                return 0

            lax.fori_loop(0, fours, four, 0)
            left = high - low - 4 * fours

            @pl.when(left >= 2)
            def _():
                several(high - left, 2)

            @pl.when((left == 1) | (left == 3))
            def _():
                several(high - 1, 1)

            if last:
                keep_own, send_own, keep_end, send_end = outs
                half = tokens // 2
                first_group = who_ref[GROUP] == 0
                for own_rows, keep_ref, send_ref in (
                    (True, keep_own, send_own),
                    (False, keep_end, send_end),
                ):

                    @pl.when((turn < heads) == own_rows)
                    def _(keep_ref=keep_ref, send_ref=send_ref):
                        for member in range(rows // tokens):
                            lanes = pl.ds(member * tokens, tokens)
                            result = accum_ref[turn, :, lanes] / total_ref[turn, :, lanes]
                            result = result.T
                            top, bottom = result[:half], result[half:]
                            column = pl.ds(
                                pl.multiple_of((head * (rows // tokens) + member) * width, width), width
                            )
                            keep_ref[:, column] = jnp.where(first_group, top, bottom).astype(jnp.bfloat16)
                            send_ref[:, column] = jnp.where(first_group, bottom, top).astype(jnp.bfloat16)

            return 0

        for lowest, highest, stage, tiles, fresh in parts:
            body = functools.partial(
                one_turn, group=0 if lowest < heads else 1, stage=stage, tiles=tiles, fresh=fresh
            )
            lax.fori_loop(lowest, highest, body, 0)
        if not last:
            stores = []
            for number, (lowest, highest, _, _, _) in enumerate(parts):
                here = pl.ds(lowest, highest - lowest)
                stores += [
                    pltpu.make_async_copy(ref.at[here], out.at[here], state_sems.at[number, at])
                    for at, (ref, out) in enumerate(zip(state_refs, outs))
                ]
            for store in stores:
                store.start()
            for store in stores:
                store.wait()


def attend_call(scale, chunks, who, counts, tokens, parts, queries, buffers, state, tiles=None, last=False):
    layout = tuple(buffer[:3] + (buffer[4],) for buffer in buffers)
    arrays = [buffer[3] for buffer in buffers]
    _, width, rows = queries[0].shape
    n_turn = 2 * (counts.shape[0] // 4)
    heads = counts.shape[0] // 4
    n_units = sum(array.shape[0] - buffer[2] for array, buffer in zip(arrays, buffers))
    state_shapes = [(n_turn, 1, rows), (n_turn, 1, rows), (n_turn, width, rows)]
    if last:
        outs = [jax.ShapeDtypeStruct((tokens // 2, heads * (rows // tokens) * width), jnp.bfloat16)] * 4
    else:
        outs = [jax.ShapeDtypeStruct(shape, jnp.float32) for shape in state_shapes]
    given = [] if state is None else list(state)
    tile_args = [] if tiles is None else list(tiles)
    before = 2 + len(queries) + len(arrays) + len(tile_args)
    aliases = {} if last or state is None else {before + at: at for at in range(3)}
    return pl.pallas_call(
        functools.partial(
            attend_kernel,
            scale,
            chunks,
            layout,
            len(queries),
            tuple(parts),
            len(given),
            last,
        ),
        out_shape=tuple(outs),
        in_specs=[smem(), smem()]
        + [hbm()] * (len(queries) + len(arrays))
        + [vmem()] * len(tile_args)
        + [hbm()] * len(given),
        out_specs=tuple([vmem() if last else hbm()] * len(outs)),
        scratch_shapes=[pltpu.VMEM((n_turn, width, rows), jnp.bfloat16)]
        + [pltpu.VMEM(shape, jnp.float32) for shape in state_shapes]
        + [
            pltpu.VMEM((n_units,) + arrays[0].shape[1:], jnp.bfloat16),
            pltpu.SemaphoreType.DMA((n_units,)),
            pltpu.SemaphoreType.DMA((len(parts), 3)),
            pltpu.SemaphoreType.DMA((len(queries),)),
        ],
        input_output_aliases=aliases,
        compiler_params=pltpu.CompilerParams(vmem_limit_bytes=VMEM),
        cost_estimate=TINY,
    )(who, counts, *queries, *arrays, *tile_args, *given)


def line_of_four(query, new_keys, new_values, memory_keys, memory_values, retrieved):
    queries = query[0]
    tokens, heads, group_size, width = queries.shape
    units_dev = memory_keys.shape[0]
    scale = math.log2(math.e) / math.sqrt(width)
    me = lax.axis_index("mem")
    span = lax.axis_index("span")
    group = lax.axis_index("head")
    low = (me < 2).astype(jnp.int32)
    middle = (me == 1) | (me == 2)
    end = jnp.where(low == 1, 0, 3)
    who = jnp.stack([me, end, 3 - me, 3 - end, low, span > 0, middle, group]).astype(jnp.int32)

    def inward(value):
        return lax.ppermute(value, "mem", [(0, 1), (3, 2)])

    def across(value):
        return lax.ppermute(value, "mem", [(1, 2), (2, 1)])

    def far(value):
        return lax.ppermute(value, "mem", [(0, 2), (3, 1)])

    def onward(value):
        return lax.ppermute(value, "span", [(at, at + 1) for at in range(lax.axis_size("span") - 1)])

    n_mem = lax.axis_size("mem")

    def after(value, before):
        return lax.optimization_barrier((value, before))[0]

    half = heads // 2

    def query_t(value):
        return jnp.transpose(value, (1, 3, 2, 0)).reshape(-1, width, group_size * tokens)

    own_t = [query_t(queries[:, :half])]
    early = inward(own_t[0])
    keys = memory_keys.reshape(units_dev, -1, width)
    values = memory_values.reshape(units_dev, -1, width)
    tile_pair = (new_keys[0].reshape(-1, width), new_values[0].reshape(-1, width))
    unit_lists = after(retrieved[0], own_t[0])
    counts, table, own_0 = gather(who, unit_lists, keys, values, PIECES[:1], 0, tile=tile_pair, n_owner=n_mem)
    stream_0, end_0 = across(own_0), inward(after(own_0, early))
    tile = own_0[:TILE]
    far_tile = far(tile)
    (own_1,) = gather(who, unit_lists, keys, values, PIECES[1:], PIECES[0], table=table)
    end_1 = inward(own_1)
    own_t.append(query_t(after(queries[:, half:], own_1)))
    late = inward(after(own_t[1], end_0))

    places = [sum(PIECES[:at]) for at in range(len(PIECES))]
    starts = [sum(CHUNKS[:at]) for at in range(len(CHUNKS))]
    own = [(OWN, places[0], TILE, own_0), (OWN, places[1], 0, own_1)]
    ends = [(END, places[0], TILE, end_0), (END, places[1], 0, end_1)]
    streams = [(STREAM, starts[0], TILE, stream_0)]
    call = functools.partial(attend_call, scale, CHUNKS, who, counts, tokens)

    def send_chunk(at, sources, state):
        sources = [source[:3] + (after(source[3], state[0]),) for source in sources]
        packed = pack(who, counts, heads, CHUNKS, starts[at], CHUNKS[at], sources)
        streams.append((STREAM, starts[at], 0, across(packed)))
        return [after(state[0], packed), *state[1:]]

    def stage(buffers, before=None):
        if before is not None:
            buffers = [buffer[:3] + (after(buffer[3], before[0]),) for buffer in buffers]
        return [buffer + (0,) for buffer in buffers]

    def parts(tiles, fresh):
        return [(0, heads, 0, tiles, fresh), (heads, 2 * heads, 0, tiles, fresh)]

    mine, first, second = (0, heads), (heads, heads + half), (heads + half, 2 * heads)
    def pinned(buffers, before):
        return [buffer[:3] + (after(buffer[3], before[0]),) for buffer in buffers]

    by_owner = counts.reshape(-1, heads).sum(axis=1)
    over = jnp.maximum(by_owner[0] + by_owner[1], by_owner[2] + by_owner[3]) > sum(CHUNKS)
    own_t[0] = after(own_t[0], over)
    state = list(call([mine + (0, False, True), first + (0, False, True)], own_t + [early], stage(own), None))
    state = send_chunk(1, own[1:] + ends[:1], state)
    state = list(
        call(
            [mine + (0, False, False), first + (0, False, False)],
            own_t + [early],
            stage(streams[:1] + ends[:1], state),
            state,
        )
    )
    tiles = jnp.concatenate([own_0[:TILE], end_0[:TILE], stream_0[:TILE], after(far_tile, state[0])])
    tiles = (tiles, onward(tiles))
    state = send_chunk(2, own[1:] + ends, state)
    state = list(
        call(
            [mine + (0, True, False), first + (0, True, False)],
            own_t + [early],
            stage(ends[1:] + streams[1:2], state),
            state, tiles=tiles,
        )
    )
    late = after(late, state[0])
    both_t = own_t + [early, late]
    waiting = stage(own + streams[:1] + ends + streams[1:2], state)
    last_streams = [buffer + (1,) for buffer in streams[2:]]
    final = functools.partial(
        call,
        [mine + (1, False, False), first + (1, False, False), second + (0, True, True)],
        both_t,
        tiles=tiles,
        last=True,
    )

    def fits(piece, state):
        return final(waiting + last_streams, state)

    def exceeds(piece, state):
        return final(waiting + last_streams + [(EXTRA, places[-1], 0, across(piece), 1)], state)

    keep_own, send_own, keep_end, send_end = lax.cond(over, exceeds, fits, own_1, tuple(state))

    n_head = lax.axis_size("head")

    def pairs(moves):
        return [
            (source * n_head + at, target * n_head + (at + turn) % n_head)
            for source, target, turn in moves
            for at in range(n_head)
        ]

    axes = ("mem", "head")
    kept = lax.ppermute(keep_end, axes, pairs([(1, 0, 0), (2, 3, 0)]))
    swapped_end = lax.ppermute(send_end, axes, pairs([(1, 0, 1), (2, 3, 1)]))
    swapped_own = lax.ppermute(send_own, axes, pairs([(1, 1, 1), (2, 2, 1)]))
    same = jnp.where(middle, keep_own, kept)
    other = jnp.where(middle, swapped_own, swapped_end)
    left = jnp.where(group == 0, same, other)
    right = jnp.where(group == 0, other, same)
    return jnp.concatenate([left, right], axis=1)[None]


def shifted(value, axis, steps):
    count = lax.axis_size(axis)
    first, last = (max(0, -steps), min(count, count - steps))
    return lax.ppermute(value, axis, [(source, source + steps) for source in range(first, last)])


def any_line(query, new_keys, new_values, memory_keys, memory_values, retrieved):
    queries = query[0]
    row_count, head_count, group_size, head_width = queries.shape
    score_scale = 1.0 / math.sqrt(head_width)
    mem_index = lax.axis_index("mem")
    block_index = lax.axis_index("span")
    row_position = mem_index * row_count + jnp.arange(row_count, dtype=jnp.int32)

    def update(carry_state, key_pair, key_mask):
        old_peak, old_total, old_accum = carry_state
        scores = (
            jnp.einsum("rhgd,khd->rhgk", queries, key_pair[0], preferred_element_type=jnp.float32)
            * score_scale
        )
        scores = jnp.where(key_mask, scores, NEG)
        new_peak = jnp.maximum(old_peak, jnp.max(scores, axis=-1))
        weights = jnp.where(key_mask, jnp.exp(scores - new_peak[..., None]), 0.0)
        factor = jnp.exp(old_peak - new_peak)
        new_total = old_total * factor + jnp.sum(weights, axis=-1)
        new_accum = old_accum * factor[..., None] + jnp.einsum(
            "rhgk,khd->rhgd",
            weights.astype(jnp.bfloat16),
            key_pair[1],
            preferred_element_type=jnp.float32,
        )
        return (new_peak, new_total, new_accum)

    def sweep(carry_state, key_pair, first_key, mask_maker):
        key_count = key_pair.shape[1]
        step_size = key_count if key_count <= 1024 else math.gcd(key_count, 512)

        def advance(step_index, loop_state):
            sub_pair = lax.dynamic_slice_in_dim(key_pair, step_index * step_size, step_size, 1)
            key_position = (
                first_key + step_index * step_size + jnp.arange(step_size, dtype=jnp.int32)
            )
            return update(loop_state, sub_pair, mask_maker(key_position))

        return lax.fori_loop(0, key_count // step_size, advance, carry_state)

    def current_mask(key_position):
        return (key_position[None, :] <= row_position[:, None])[:, None, None, :]

    def prior_mask(key_position):
        return ((key_position[None, :] > row_position[:, None]) & (block_index > 0))[
            :, None, None, :
        ]

    def full_mask(key_position):
        return jnp.ones((1, 1, 1, key_position.shape[0]), bool)

    carry_state = (
        jnp.full((row_count, head_count, group_size), NEG, jnp.float32),
        jnp.zeros((row_count, head_count, group_size), jnp.float32),
        jnp.zeros((row_count, head_count, group_size, head_width), jnp.float32),
    )
    own_pair = jnp.stack([new_keys[0], new_values[0]])
    prior_pair = shifted(own_pair, "span", 1)
    loop_state = carry_state
    first_key = jnp.int32(0)
    loop_state = sweep(
        loop_state, lax.all_gather(own_pair, "mem", axis=1, tiled=True), first_key, current_mask
    )
    carry_state = sweep(
        loop_state, lax.all_gather(prior_pair, "mem", axis=1, tiled=True), first_key, prior_mask
    )
    unit_lists = retrieved[0]
    units_dev = memory_keys.shape[0]
    owners = unit_lists // units_dev
    local_units = unit_lists % units_dev
    owned_here = owners == mem_index
    gathered_pair = []
    for source_array in (memory_keys, memory_values):
        per_head = [
            source_array[local_units[head_at], :, head_at, :] for head_at in range(head_count)
        ]
        gathered_pair.append(jnp.stack(per_head, axis=2))
    gathered_units = jnp.stack(gathered_pair)
    keep_mask = jnp.transpose(owned_here)[None, :, None, :, None]
    slot_terms = jnp.where(keep_mask, gathered_units, jnp.zeros((), jnp.bfloat16))
    slot_terms = slot_terms.reshape(2, -1, head_count, head_width)
    summed_pair = lax.psum(slot_terms, "mem").astype(jnp.float32).astype(jnp.bfloat16)
    carry_state = sweep(carry_state, summed_pair, 0, full_mask)
    final_peak, final_total, final_accum = carry_state
    attended = (final_accum / final_total[..., None]).astype(jnp.bfloat16)
    attended = attended.reshape(row_count, head_count * group_size * head_width)
    moved = lax.all_to_all(attended, "head", split_axis=0, concat_axis=1, tiled=True)
    return moved[None]


def solution(mesh):
    local = line_of_four if mesh.shape["mem"] == 4 and mesh.shape["head"] == 2 else any_line
    return jax.shard_map(
        local,
        mesh=mesh,
        in_specs=(
            P("span", "mem", "head", None, None),
            P("span", "mem", "head", None),
            P("span", "mem", "head", None),
            P("mem", None, "head", None),
            P("mem", None, "head", None),
            P("span", "head", None),
        ),
        out_specs=P("span", ("mem", "head"), None),
        check_vma=False,
    )
```

```python
import functools
import math

import jax
import jax.numpy as jnp
from jax import lax
from jax.experimental import pallas as pl
from jax.experimental.pallas import tpu as pltpu
from jax.sharding import PartitionSpec as P

NEG = -1e30
LANES = 128
VMEM = 56 * 1024 * 1024
TINY = pl.CostEstimate(flops=1000, bytes_accessed=1000, transcendentals=0)
AHEAD = 6

PIECES = (16, 16)
CHUNKS = (16, 16, 16)
FIRST = 16
TILE = 4

ME, ENDER, OPPOSITE, FAR, LOW, PRIOR, MIDDLE, GROUP = range(8)
OWN, END, STREAM, EXTRA = range(4)


def smem():
    return pl.BlockSpec(memory_space=pltpu.SMEM)


def vmem():
    return pl.BlockSpec(memory_space=pltpu.VMEM)


def hbm():
    return pl.BlockSpec(memory_space=pl.ANY)


def head_picker(tokens, rows, head):
    token = lax.broadcasted_iota(jnp.int32, (tokens, rows), 0)
    row = lax.broadcasted_iota(jnp.int32, (tokens, rows), 1)
    return (row == token * (rows // tokens) + head).astype(jnp.bfloat16)


def pick_pair(pick, keys, values):
    keys = jnp.dot(pick, keys, preferred_element_type=jnp.float32)
    values_t = lax.dot_general(
        values, pick, (((0,), (1,)), ((), ())), preferred_element_type=jnp.float32
    )
    return keys.astype(jnp.bfloat16), values_t.astype(jnp.bfloat16)


def plan_units(units_dev, who_ref, list_ref, count_ref, table_ref):
    heads, topk = list_ref.shape
    me = who_ref[ME]

    def clear(at, _):
        count_ref[at] = 0
        return 0

    lax.fori_loop(0, count_ref.shape[0], clear, 0)
    used = jnp.int32(0)
    for head in range(heads):

        def note(at, used, head=head):
            unit = list_ref[head, at]
            owner = lax.div(unit, jnp.int32(units_dev))
            entry = owner * heads + head
            count_ref[entry] = count_ref[entry] + 1
            table_ref[used] = (unit - owner * units_dev) * heads + head
            return used + (owner == me).astype(jnp.int32)

        used = lax.fori_loop(0, topk, note, used)
    table_ref[heads * topk] = used


def gather_kernel(units_dev, pieces, first, tile, who_ref, list_ref, keys_ref, values_ref, *refs):
    refs = list(refs)
    heads, topk = list_ref.shape
    if tile:
        new_keys, new_values, count_ref, table_ref = (refs.pop(0) for _ in range(4))
        plan_units(units_dev, who_ref, list_ref, count_ref, table_ref)
    else:
        table_ref = refs.pop(0)
    outs = [refs.pop(0) for _ in pieces]
    key_buf, value_buf, picks, sems = refs
    rows = keys_ref.shape[1]
    tokens = rows // heads
    used = table_ref[heads * topk]

    def copies(at):
        unit = lax.div(table_ref[at], jnp.int32(heads))
        slot = lax.rem(at, jnp.int32(AHEAD))
        return (
            pltpu.make_async_copy(keys_ref.at[unit], key_buf.at[slot], sems.at[slot, 0]),
            pltpu.make_async_copy(values_ref.at[unit], value_buf.at[slot], sems.at[slot, 1]),
        )

    def start(at, _):
        for copy in copies(at):
            copy.start()
        return 0

    stop = jnp.minimum(used, first + sum(pieces))
    lax.fori_loop(first, jnp.minimum(stop, first + AHEAD), start, 0)
    for head in range(heads):
        picks[head] = head_picker(tokens, rows, head)
    base, place = first, TILE if tile else 0
    if tile:
        for head in range(heads):
            outs[0][head, 0], outs[0][head, 1] = pick_pair(picks[head], new_keys[...], new_values[...])
    for out_ref, size in zip(outs, pieces):

        def item(slot, _, out_ref=out_ref, base=base, place=place):
            at = base + slot
            for copy in copies(at):
                copy.wait()
            here = lax.rem(at, jnp.int32(AHEAD))
            pick = picks[lax.rem(table_ref[at], jnp.int32(heads))]
            out_ref[place + slot, 0], out_ref[place + slot, 1] = pick_pair(
                pick, key_buf[here], value_buf[here]
            )

            @pl.when(at + AHEAD < stop)
            def _():
                start(at + AHEAD, 0)

            return 0

        lax.fori_loop(0, jnp.clip(used - base, 0, size), item, 0)
        base, place = base + size, 0


def gather(who, unit_lists, keys, values, pieces, first, tile=None, table=None, n_owner=None):
    units, rows, width = keys.shape
    heads, topk = unit_lists.shape
    tokens = rows // heads
    extra = [TILE if tile is not None else 0] + [0] * (len(pieces) - 1)
    tables = [
        jax.ShapeDtypeStruct((size,), jnp.int32)
        for size in ([n_owner * heads, heads * topk + 1] if tile is not None else [])
    ]
    return pl.pallas_call(
        functools.partial(gather_kernel, units, pieces, first, tile is not None),
        out_shape=tuple(
            tables
            + [
                jax.ShapeDtypeStruct((size + more, 2, tokens, width), jnp.bfloat16)
                for size, more in zip(pieces, extra)
            ]
        ),
        in_specs=[smem(), smem(), hbm(), hbm()] + ([vmem()] * 2 if tile is not None else [smem()]),
        out_specs=tuple([smem()] * len(tables) + [vmem()] * len(pieces)),
        scratch_shapes=[
            pltpu.VMEM((AHEAD, rows, width), jnp.bfloat16),
            pltpu.VMEM((AHEAD, rows, width), jnp.bfloat16),
            pltpu.VMEM((heads, tokens, rows), jnp.bfloat16),
            pltpu.SemaphoreType.DMA((AHEAD, 2)),
        ],
        compiler_params=pltpu.CompilerParams(vmem_limit_bytes=VMEM),
        cost_estimate=TINY,
    )(who, unit_lists, keys, values, *(tile if tile is not None else (table,)))


def head_ranges(count_ref, heads, owner):
    ranges, at = [], jnp.int32(0)
    for head in range(heads):
        after = at + count_ref[owner * heads + head]
        ranges.append((at, after))
        at = after
    return ranges, at


def stream_shape(chunks, n_middle, n_end):
    extra = jnp.maximum(n_middle + n_end - sum(chunks), 0)
    return extra, jnp.maximum(n_middle - extra, FIRST)


def pack_kernel(heads, chunks, first, layout, who_ref, count_ref, *refs):
    sources = refs[: len(layout)]
    out_ref, sems = refs[len(layout) :]
    size = out_ref.shape[0]

    @pl.when(who_ref[MIDDLE] == 1)
    def _():
        _, n_own = head_ranges(count_ref, heads, who_ref[ME])
        _, n_end = head_ranges(count_ref, heads, who_ref[ENDER])
        extra, base = stream_shape(chunks, n_own, n_end)

        def each(act):
            for (kind, at, skip), ref in zip(layout, sources):
                shift, total = (-extra, n_own) if kind == OWN else (base, n_end)
                count = ref.shape[0] - skip
                low = jnp.maximum(at + shift, first)
                high = jnp.minimum(jnp.minimum(at + count, total) + shift, first + size)

                def one(slot, _, ref=ref, shift=shift, at=at, skip=skip):
                    place = slot - first
                    act(
                        pltpu.make_async_copy(
                            ref.at[slot - shift - at + skip], out_ref.at[place], sems.at[place]
                        )
                    )
                    return 0

                lax.fori_loop(low, jnp.maximum(low, high), one, 0)

        each(lambda copy: copy.start())
        each(lambda copy: copy.wait())


def pack(who, counts, heads, chunks, first, size, sources):
    layout = tuple(source[:3] for source in sources)
    arrays = [source[3] for source in sources]
    return pl.pallas_call(
        functools.partial(pack_kernel, heads, chunks, first, layout),
        out_shape=jax.ShapeDtypeStruct((size,) + arrays[0].shape[1:], jnp.bfloat16),
        in_specs=[smem(), smem()] + [hbm()] * len(arrays),
        out_specs=vmem(),
        scratch_shapes=[pltpu.SemaphoreType.DMA((size,))],
        compiler_params=pltpu.CompilerParams(vmem_limit_bytes=VMEM),
        cost_estimate=TINY,
    )(who, counts, *arrays)


def attend(scale, keys, values_t, queries_t, mask, state):
    peak, total, accum = state
    scores = jnp.dot(keys, queries_t, preferred_element_type=jnp.float32)
    if mask is not None:
        scores = jnp.where(mask, scores, NEG)
    new_peak = jnp.maximum(peak, jnp.max(scores, axis=0, keepdims=True))
    weights = jnp.exp2((scores - new_peak) * scale)
    factor = jnp.exp2((peak - new_peak) * scale)
    total = total * factor + jnp.sum(weights, axis=0, keepdims=True)
    accum = accum * factor + jnp.dot(
        values_t, weights.astype(jnp.bfloat16), preferred_element_type=jnp.float32
    )
    return new_peak, total, accum


def attend_kernel(scale, chunks, layout, n_query, parts, n_state, last, *refs):
    new = any(part[3] for part in parts)
    refs = list(refs)
    who_ref, count_ref = refs.pop(0), refs.pop(0)
    query_in = [refs.pop(0) for _ in range(n_query)]
    buffers = [refs.pop(0) for _ in layout]
    if new:
        cur, prior = refs.pop(0), refs.pop(0)
    state_in = [refs.pop(0) for _ in range(n_state)]
    outs = [refs.pop(0) for _ in range(4 if last else 3)]
    queries, peak_ref, total_ref, accum_ref, units, unit_sems, state_sems, query_sems = refs
    state_refs = (peak_ref, total_ref, accum_ref)
    n_turn, width, rows = queries.shape
    tokens = units.shape[2]
    heads = list(count_ref.shape)[0] // 4

    def update(turn, keys, values_t, mask=None):
        for start in range(0, rows, LANES):
            lanes = pl.ds(start, LANES)
            state = tuple(ref[turn, :, lanes] for ref in state_refs)
            state = attend(scale, keys, values_t, queries[turn, :, lanes], mask, state)
            for ref, part in zip(state_refs, state):
                ref[turn, :, lanes] = part

    def new_tiles(turn, head, group):
        low, has_prior = who_ref[LOW] == 1, who_ref[PRIOR] == 1

        def tile(ref, at=0):
            return ref[at * TILE + head, 0], ref[at * TILE + head, 1]

        def choose(flag, yes, no):
            return tuple(jnp.where(flag, a, b) for a, b in zip(yes, no))

        def join(a, b):
            return jnp.concatenate([a[0], b[0]], axis=0), jnp.concatenate([a[1], b[1]], axis=1)

        key = lax.broadcasted_iota(jnp.int32, (2 * tokens, LANES), 0)
        position = lax.broadcasted_iota(jnp.int32, (2 * tokens, LANES), 1) % tokens
        mask = ((key < tokens) & (key <= position)) | (
            (key >= tokens) & (key - tokens > position) & has_prior
        )

        def both():
            pairs = [choose(low, tile(prior, at), tile(cur, at)) for at in (2, 3)]
            update(turn, *join(*pairs))

        if group == 0:
            update(turn, *join(tile(cur), tile(prior)), mask)

            @pl.when(low | has_prior)
            def _():
                update(turn, *choose(low, tile(cur, 1), tile(prior, 1)))

            pl.when(jnp.logical_not(low) | has_prior)(both)
        else:
            update(turn, *join(tile(cur, 1), tile(prior, 1)), mask)

            @pl.when(jnp.logical_not(low) | has_prior)
            def _():
                update(turn, *choose(low, tile(prior), tile(cur)))
                both()

    @pl.when(who_ref[MIDDLE] == 1)
    def _():
        loads = []
        at = parts[0][0]
        for number, ref in enumerate(query_in):
            here = pl.ds(at, ref.shape[0])
            loads.append(pltpu.make_async_copy(ref, queries.at[here], query_sems.at[number]))
            at += ref.shape[0]
        for number, (lowest, highest, _, _, fresh) in enumerate(parts):
            if not fresh:
                here = pl.ds(lowest, highest - lowest)
                loads += [
                    pltpu.make_async_copy(source.at[here], ref.at[here], state_sems.at[number, at])
                    for at, (source, ref) in enumerate(zip(state_in, state_refs))
                ]
        for load in loads:
            load.start()

        ranges, totals = zip(
            *(head_ranges(count_ref, heads, who_ref[role]) for role in (ME, ENDER, OPPOSITE, FAR))
        )
        extra, base = stream_shape(chunks, totals[2], totals[3])
        n_stage = max(entry[3] for entry in layout) + 1
        place, bounds = jnp.int32(0), []
        for head in range(heads):
            stage_at = -1
            for (kind, first, skip, stage), buffer in zip(layout, buffers):
                while stage_at < stage:
                    stage_at += 1
                    bounds.append(place)
                if kind == STREAM:
                    low, high = ranges[2][head]
                    spans = [
                        (low, jnp.minimum(high, FIRST)),
                        (jnp.maximum(low, FIRST + extra) - extra, high - extra),
                    ]
                    low, high = ranges[3][head]
                    spans.append((base + low, base + high))
                elif kind == EXTRA:
                    low, high = ranges[2][head]
                    spans = [(jnp.maximum(low, FIRST), jnp.minimum(high, FIRST + extra))]
                else:
                    spans = [ranges[0 if kind == OWN else 1][head]]
                for low, high in spans:
                    low = jnp.maximum(low - first, 0)
                    high = jnp.maximum(jnp.minimum(high - first, buffer.shape[0] - skip), low)

                    def fetch(at, _, buffer=buffer, skip=skip, shift=place - low):
                        slot = at + shift
                        pltpu.make_async_copy(
                            buffer.at[at + skip], units.at[slot], unit_sems.at[slot]
                        ).start()
                        return 0

                    lax.fori_loop(low, high, fetch, 0)
                    place = place + high - low
            bounds.append(place)

        def arrived(slot, _):
            pltpu.make_async_copy(buffers[0].at[0], units.at[slot], unit_sems.at[slot]).wait()
            return 0

        lax.fori_loop(0, place, arrived, 0)
        for load in loads:
            load.wait()

        def one_turn(turn, _, group, stage, tiles, fresh):
            head = lax.rem(turn, jnp.int32(heads))
            if fresh:
                peak_ref[turn] = jnp.full((1, rows), NEG, jnp.float32)
                total_ref[turn] = jnp.zeros((1, rows), jnp.float32)
                accum_ref[turn] = jnp.zeros((width, rows), jnp.float32)
            if tiles:
                new_tiles(turn, head, group)
            low, high = jnp.int32(0), jnp.int32(0)
            for at in range(heads):
                low = jnp.where(head == at, bounds[at * (n_stage + 1) + stage], low)
                high = jnp.where(head == at, bounds[at * (n_stage + 1) + n_stage], high)

            def several(slot, count):
                keys = units[pl.ds(slot, count), 0].reshape(count * tokens, width)
                values_t = jnp.concatenate([units[slot + at, 1] for at in range(count)], axis=1)
                update(turn, keys, values_t)

            fours = lax.div(high - low, jnp.int32(4))

            def four(at, _):
                several(low + 4 * at, 4)
                return 0

            lax.fori_loop(0, fours, four, 0)
            left = high - low - 4 * fours

            @pl.when(left >= 2)
            def _():
                several(high - left, 2)

            @pl.when((left == 1) | (left == 3))
            def _():
                several(high - 1, 1)

            if last:
                keep_own, send_own, keep_end, send_end = outs
                half = tokens // 2
                first_group = who_ref[GROUP] == 0
                for own_rows, keep_ref, send_ref in (
                    (True, keep_own, send_own),
                    (False, keep_end, send_end),
                ):

                    @pl.when((turn < heads) == own_rows)
                    def _(keep_ref=keep_ref, send_ref=send_ref):
                        for member in range(rows // tokens):
                            lanes = pl.ds(member * tokens, tokens)
                            result = accum_ref[turn, :, lanes] / total_ref[turn, :, lanes]
                            result = result.T
                            top, bottom = result[:half], result[half:]
                            column = pl.ds(
                                pl.multiple_of((head * (rows // tokens) + member) * width, width), width
                            )
                            keep_ref[:, column] = jnp.where(first_group, top, bottom).astype(jnp.bfloat16)
                            send_ref[:, column] = jnp.where(first_group, bottom, top).astype(jnp.bfloat16)

            return 0

        for lowest, highest, stage, tiles, fresh in parts:
            body = functools.partial(
                one_turn, group=0 if lowest < heads else 1, stage=stage, tiles=tiles, fresh=fresh
            )
            lax.fori_loop(lowest, highest, body, 0)
        if not last:
            stores = []
            for number, (lowest, highest, _, _, _) in enumerate(parts):
                here = pl.ds(lowest, highest - lowest)
                stores += [
                    pltpu.make_async_copy(ref.at[here], out.at[here], state_sems.at[number, at])
                    for at, (ref, out) in enumerate(zip(state_refs, outs))
                ]
            for store in stores:
                store.start()
            for store in stores:
                store.wait()


def attend_call(scale, chunks, who, counts, tokens, parts, queries, buffers, state, tiles=None, last=False):
    layout = tuple(buffer[:3] + (buffer[4],) for buffer in buffers)
    arrays = [buffer[3] for buffer in buffers]
    _, width, rows = queries[0].shape
    n_turn = 2 * (counts.shape[0] // 4)
    heads = counts.shape[0] // 4
    n_units = sum(array.shape[0] - buffer[2] for array, buffer in zip(arrays, buffers))
    state_shapes = [(n_turn, 1, rows), (n_turn, 1, rows), (n_turn, width, rows)]
    if last:
        outs = [jax.ShapeDtypeStruct((tokens // 2, heads * (rows // tokens) * width), jnp.bfloat16)] * 4
    else:
        outs = [jax.ShapeDtypeStruct(shape, jnp.float32) for shape in state_shapes]
    given = [] if state is None else list(state)
    tile_args = [] if tiles is None else list(tiles)
    before = 2 + len(queries) + len(arrays) + len(tile_args)
    aliases = {} if last or state is None else {before + at: at for at in range(3)}
    return pl.pallas_call(
        functools.partial(
            attend_kernel,
            scale,
            chunks,
            layout,
            len(queries),
            tuple(parts),
            len(given),
            last,
        ),
        out_shape=tuple(outs),
        in_specs=[smem(), smem()]
        + [hbm()] * (len(queries) + len(arrays))
        + [vmem()] * len(tile_args)
        + [hbm()] * len(given),
        out_specs=tuple([vmem() if last else hbm()] * len(outs)),
        scratch_shapes=[pltpu.VMEM((n_turn, width, rows), jnp.bfloat16)]
        + [pltpu.VMEM(shape, jnp.float32) for shape in state_shapes]
        + [
            pltpu.VMEM((n_units,) + arrays[0].shape[1:], jnp.bfloat16),
            pltpu.SemaphoreType.DMA((n_units,)),
            pltpu.SemaphoreType.DMA((len(parts), 3)),
            pltpu.SemaphoreType.DMA((len(queries),)),
        ],
        input_output_aliases=aliases,
        compiler_params=pltpu.CompilerParams(vmem_limit_bytes=VMEM),
        cost_estimate=TINY,
    )(who, counts, *queries, *arrays, *tile_args, *given)


def join_kernel(who_ref, keep_own, kept, swapped_own, swapped_end, out_ref, sems):
    width = keep_own.shape[1]
    for middle, same, other in ((1, keep_own, swapped_own), (0, kept, swapped_end)):
        for group in range(2):

            @pl.when((who_ref[MIDDLE] == middle) & (who_ref[GROUP] == group))
            def _(same=same, other=other, group=group):
                copies = [
                    pltpu.make_async_copy(part, out_ref.at[:, pl.ds(at * width, width)], sems.at[at])
                    for at, part in ((group, same), (1 - group, other))
                ]
                for copy in copies:
                    copy.start()
                for copy in copies:
                    copy.wait()


def join_rows(who, *parts):
    rows, width = parts[0].shape
    return pl.pallas_call(
        join_kernel,
        out_shape=jax.ShapeDtypeStruct((rows, 2 * width), parts[0].dtype),
        in_specs=[smem()] + [hbm()] * 4,
        out_specs=vmem(),
        scratch_shapes=[pltpu.SemaphoreType.DMA((2,))],
        compiler_params=pltpu.CompilerParams(vmem_limit_bytes=VMEM),
        cost_estimate=TINY,
    )(who, *parts)


def line_of_four(query, new_keys, new_values, memory_keys, memory_values, retrieved):
    queries = query[0]
    tokens, heads, group_size, width = queries.shape
    units_dev = memory_keys.shape[0]
    scale = math.log2(math.e) / math.sqrt(width)
    me = lax.axis_index("mem")
    span = lax.axis_index("span")
    group = lax.axis_index("head")
    low = (me < 2).astype(jnp.int32)
    middle = (me == 1) | (me == 2)
    end = jnp.where(low == 1, 0, 3)
    who = jnp.stack([me, end, 3 - me, 3 - end, low, span > 0, middle, group]).astype(jnp.int32)

    def inward(value):
        return lax.ppermute(value, "mem", [(0, 1), (3, 2)])

    def across(value):
        return lax.ppermute(value, "mem", [(1, 2), (2, 1)])

    def far(value):
        return lax.ppermute(value, "mem", [(0, 2), (3, 1)])

    def onward(value):
        return lax.ppermute(value, "span", [(at, at + 1) for at in range(lax.axis_size("span") - 1)])

    n_mem = lax.axis_size("mem")

    def after(value, before):
        return lax.optimization_barrier((value, before))[0]

    half = heads // 2

    def query_t(value):
        return jnp.transpose(value, (1, 3, 2, 0)).reshape(-1, width, group_size * tokens)

    own_t = [query_t(queries[:, :half])]
    early = inward(own_t[0])
    keys = memory_keys.reshape(units_dev, -1, width)
    values = memory_values.reshape(units_dev, -1, width)
    tile_pair = (new_keys[0].reshape(-1, width), new_values[0].reshape(-1, width))
    unit_lists = after(retrieved[0], own_t[0])
    counts, table, own_0 = gather(who, unit_lists, keys, values, PIECES[:1], 0, tile=tile_pair, n_owner=n_mem)
    stream_0, end_0 = across(own_0), inward(after(own_0, early))
    tile = own_0[:TILE]
    far_tile = far(tile)
    (own_1,) = gather(who, unit_lists, keys, values, PIECES[1:], PIECES[0], table=table)
    end_1 = inward(own_1)
    own_t.append(query_t(after(queries[:, half:], own_1)))
    late = inward(after(own_t[1], end_0))

    places = [sum(PIECES[:at]) for at in range(len(PIECES))]
    starts = [sum(CHUNKS[:at]) for at in range(len(CHUNKS))]
    own = [(OWN, places[0], TILE, own_0), (OWN, places[1], 0, own_1)]
    ends = [(END, places[0], TILE, end_0), (END, places[1], 0, end_1)]
    streams = [(STREAM, starts[0], TILE, stream_0)]
    call = functools.partial(attend_call, scale, CHUNKS, who, counts, tokens)

    def send_chunk(at, sources, state):
        sources = [source[:3] + (after(source[3], state[0]),) for source in sources]
        packed = pack(who, counts, heads, CHUNKS, starts[at], CHUNKS[at], sources)
        streams.append((STREAM, starts[at], 0, across(packed)))
        return [after(state[0], packed), *state[1:]]

    def stage(buffers, before=None):
        if before is not None:
            buffers = [buffer[:3] + (after(buffer[3], before[0]),) for buffer in buffers]
        return [buffer + (0,) for buffer in buffers]

    def parts(tiles, fresh):
        return [(0, heads, 0, tiles, fresh), (heads, 2 * heads, 0, tiles, fresh)]

    mine, first, second = (0, heads), (heads, heads + half), (heads + half, 2 * heads)
    def pinned(buffers, before):
        return [buffer[:3] + (after(buffer[3], before[0]),) for buffer in buffers]

    by_owner = counts.reshape(-1, heads).sum(axis=1)
    over = jnp.maximum(by_owner[0] + by_owner[1], by_owner[2] + by_owner[3]) > sum(CHUNKS)
    own_t[0] = after(own_t[0], over)
    state = list(call([mine + (0, False, True), first + (0, False, True)], own_t + [early], stage(own), None))
    state = send_chunk(1, own[1:] + ends[:1], state)
    state = list(
        call(
            [mine + (0, False, False), first + (0, False, False)],
            own_t + [early],
            stage(streams[:1] + ends[:1], state),
            state,
        )
    )
    tiles = jnp.concatenate([own_0[:TILE], end_0[:TILE], stream_0[:TILE], after(far_tile, state[0])])
    tiles = (tiles, onward(tiles))
    state = send_chunk(2, own[1:] + ends, state)
    state = list(
        call(
            [mine + (0, True, False), first + (0, True, False)],
            own_t + [early],
            stage(ends[1:] + streams[1:2], state),
            state, tiles=tiles,
        )
    )
    late = after(late, state[0])
    both_t = own_t + [early, late]
    state = list(
        call(
            [second + (0, True, True)],
            [late],
            stage(own + streams[:1] + ends + streams[1:2], state),
            state,
            tiles=tiles,
        )
    )
    last_streams = stage(streams[2:], state)
    final = functools.partial(
        call, [mine + (0, False, False), (heads, 2 * heads, 0, False, False)], both_t, last=True
    )

    def fits(piece, state):
        return final(last_streams, state)

    def exceeds(piece, state):
        return final(last_streams + [(EXTRA, places[-1], 0, across(piece), 0)], state)

    keep_own, send_own, keep_end, send_end = lax.cond(over, exceeds, fits, own_1, tuple(state))

    n_head = lax.axis_size("head")

    def pairs(moves):
        return [
            (source * n_head + at, target * n_head + (at + turn) % n_head)
            for source, target, turn in moves
            for at in range(n_head)
        ]

    axes = ("mem", "head")
    kept = lax.ppermute(keep_end, axes, pairs([(1, 0, 0), (2, 3, 0)]))
    swapped_end = lax.ppermute(send_end, axes, pairs([(1, 0, 1), (2, 3, 1)]))
    swapped_own = lax.ppermute(send_own, axes, pairs([(1, 1, 1), (2, 2, 1)]))
    return join_rows(who, keep_own, kept, swapped_own, swapped_end)[None]


def shifted(value, axis, steps):
    count = lax.axis_size(axis)
    first, last = (max(0, -steps), min(count, count - steps))
    return lax.ppermute(value, axis, [(source, source + steps) for source in range(first, last)])


def any_line(query, new_keys, new_values, memory_keys, memory_values, retrieved):
    queries = query[0]
    row_count, head_count, group_size, head_width = queries.shape
    score_scale = 1.0 / math.sqrt(head_width)
    mem_index = lax.axis_index("mem")
    block_index = lax.axis_index("span")
    row_position = mem_index * row_count + jnp.arange(row_count, dtype=jnp.int32)

    def update(carry_state, key_pair, key_mask):
        old_peak, old_total, old_accum = carry_state
        scores = (
            jnp.einsum("rhgd,khd->rhgk", queries, key_pair[0], preferred_element_type=jnp.float32)
            * score_scale
        )
        scores = jnp.where(key_mask, scores, NEG)
        new_peak = jnp.maximum(old_peak, jnp.max(scores, axis=-1))
        weights = jnp.where(key_mask, jnp.exp(scores - new_peak[..., None]), 0.0)
        factor = jnp.exp(old_peak - new_peak)
        new_total = old_total * factor + jnp.sum(weights, axis=-1)
        new_accum = old_accum * factor[..., None] + jnp.einsum(
            "rhgk,khd->rhgd",
            weights.astype(jnp.bfloat16),
            key_pair[1],
            preferred_element_type=jnp.float32,
        )
        return (new_peak, new_total, new_accum)

    def sweep(carry_state, key_pair, first_key, mask_maker):
        key_count = key_pair.shape[1]
        step_size = key_count if key_count <= 1024 else math.gcd(key_count, 512)

        def advance(step_index, loop_state):
            sub_pair = lax.dynamic_slice_in_dim(key_pair, step_index * step_size, step_size, 1)
            key_position = (
                first_key + step_index * step_size + jnp.arange(step_size, dtype=jnp.int32)
            )
            return update(loop_state, sub_pair, mask_maker(key_position))

        return lax.fori_loop(0, key_count // step_size, advance, carry_state)

    def current_mask(key_position):
        return (key_position[None, :] <= row_position[:, None])[:, None, None, :]

    def prior_mask(key_position):
        return ((key_position[None, :] > row_position[:, None]) & (block_index > 0))[
            :, None, None, :
        ]

    def full_mask(key_position):
        return jnp.ones((1, 1, 1, key_position.shape[0]), bool)

    carry_state = (
        jnp.full((row_count, head_count, group_size), NEG, jnp.float32),
        jnp.zeros((row_count, head_count, group_size), jnp.float32),
        jnp.zeros((row_count, head_count, group_size, head_width), jnp.float32),
    )
    own_pair = jnp.stack([new_keys[0], new_values[0]])
    prior_pair = shifted(own_pair, "span", 1)
    loop_state = carry_state
    first_key = jnp.int32(0)
    loop_state = sweep(
        loop_state, lax.all_gather(own_pair, "mem", axis=1, tiled=True), first_key, current_mask
    )
    carry_state = sweep(
        loop_state, lax.all_gather(prior_pair, "mem", axis=1, tiled=True), first_key, prior_mask
    )
    unit_lists = retrieved[0]
    units_dev = memory_keys.shape[0]
    owners = unit_lists // units_dev
    local_units = unit_lists % units_dev
    owned_here = owners == mem_index
    gathered_pair = []
    for source_array in (memory_keys, memory_values):
        per_head = [
            source_array[local_units[head_at], :, head_at, :] for head_at in range(head_count)
        ]
        gathered_pair.append(jnp.stack(per_head, axis=2))
    gathered_units = jnp.stack(gathered_pair)
    keep_mask = jnp.transpose(owned_here)[None, :, None, :, None]
    slot_terms = jnp.where(keep_mask, gathered_units, jnp.zeros((), jnp.bfloat16))
    slot_terms = slot_terms.reshape(2, -1, head_count, head_width)
    summed_pair = lax.psum(slot_terms, "mem").astype(jnp.float32).astype(jnp.bfloat16)
    carry_state = sweep(carry_state, summed_pair, 0, full_mask)
    final_peak, final_total, final_accum = carry_state
    attended = (final_accum / final_total[..., None]).astype(jnp.bfloat16)
    attended = attended.reshape(row_count, head_count * group_size * head_width)
    moved = lax.all_to_all(attended, "head", split_axis=0, concat_axis=1, tiled=True)
    return moved[None]


def solution(mesh):
    local = line_of_four if mesh.shape["mem"] == 4 and mesh.shape["head"] == 2 else any_line
    return jax.shard_map(
        local,
        mesh=mesh,
        in_specs=(
            P("span", "mem", "head", None, None),
            P("span", "mem", "head", None),
            P("span", "mem", "head", None),
            P("mem", None, "head", None),
            P("mem", None, "head", None),
            P("span", "head", None),
        ),
        out_specs=P("span", ("mem", "head"), None),
        check_vma=False,
    )
```
